256 devices in a mesh: tm: 32 (over y, z), col: 8 (over x, core).
Axes of the slice: x: 4, y: 4, z: 8, core: 2. Of those that a mesh axis runs over, the one named last changes fastest.
Arguments:
- diag_blocks: float32 [64, 1024, 1024], P('tm', 'col'), as said below
- lower_blocks: float32 [64, 1024, 1024], P('tm', 'col'), as said below
- obs_prec: float32 [64, 1024], P('tm', 'col'), as said below
- covariates: float32 [64, 64, 1024], P('tm', None, 'col'), may hold values from -0.0234375 to 0.0234375
- prior_prec: float32 [64, 64], replicated, as said below
Outputs:
- interior_factors: float32 [32, 1024, 1024], P('tm', 'col')
- separator_diag: float32 [32, 1024, 1024], P('tm', 'col')
- separator_coupling: float32 [32, 1024, 1024], P('tm', 'col')
- separator_arrow: float32 [32, 64, 1024], P('tm', None, 'col')
- tip_block: float32 [64, 64], replicated
- log_pivots: float32 [], replicated
The draws below stay inside these ranges and needn't reach their ends.
Inputs may be any that keep to these rules, and one draw needn't show every extreme that they name: `diag_blocks`: each block is symmetric. Together with lower_blocks, obs_prec, covariates and prior_prec it makes the matrix Q of the first step symmetric positive definite. lower_blocks[0] is not part of Q. `obs_prec`: Positive. `prior_prec`: symmetric positive definite.
All inputs are finite; a program needn't handle non-finite values.
Results may differ from the reference program's by a relative error of at most 0.00012.
Values sent between devices are 32-bit elements; how exact they have to be, the bound alone decides.
No kernel may reach another device: no remote copies, remote signals or barrier semaphores. Data moves between devices by JAX's collectives and lax.ppermute only.
A program may use at most 128 MiB of HBM per device.

```python
import math
import jax
import jax.numpy as jnp
from jax import lax

NS = 1024
NF = 64
BLOCKS_DEV = 2
NT = 64
N_TM = 32


def dense_gram(key):
    factor_rows = jax.random.uniform(key, (NS, NS), jnp.float32, -1.0, 1.0)
    product = jnp.dot(factor_rows, factor_rows.T, precision=lax.Precision.HIGHEST) / NS
    return 0.5 * (product + product.T)


def spatial_terms(key):
    gram_first = dense_gram(jax.random.fold_in(key, 101))
    gram_second = dense_gram(jax.random.fold_in(key, 104))
    scale_first = jnp.exp(jax.random.uniform(jax.random.fold_in(key, 102), (NT, NS), jnp.float32, math.log(0.7), math.log(1.4)))
    scale_second = jnp.exp(jax.random.uniform(jax.random.fold_in(key, 105), (NT, NS), jnp.float32, math.log(0.7), math.log(1.4)))
    shift_values = jax.random.uniform(jax.random.fold_in(key, 106), (NT, NS), jnp.float32, 1.5, 3.0)
    outer_first = scale_first[:, :, None] * scale_first[:, None, :]
    outer_second = scale_second[:, :, None] * scale_second[:, None, :]
    identity = jnp.eye(NS, dtype=jnp.float32)
    spatial = 6.0 * (outer_first * gram_first[None] + outer_second * gram_second[None]) + shift_values[:, :, None] * identity
    memory = jax.random.uniform(jax.random.fold_in(key, 103), (NT, NS), jnp.float32, 0.3, 0.95)
    return (spatial, memory)


def obs_terms(key):
    growth = 1.0 + 2.0 * jnp.arange(NT, dtype=jnp.float32) / max(NT - 1, 1)
    base_values = jnp.exp(jax.random.uniform(jax.random.fold_in(key, 201), (NT, NS), jnp.float32, math.log(0.25), math.log(4.0)))
    return base_values * growth[:, None]


def draw_diag_blocks(key, part):
    spatial, memory = spatial_terms(key)
    precision = obs_terms(key)
    earlier_spatial = jnp.roll(spatial, 1, axis=0)
    earlier_memory = jnp.roll(memory, 1, axis=0)
    later_mask = (jnp.arange(NT) > 0).astype(jnp.float32)[:, None, None]
    memory_outer = earlier_memory[:, :, None] * earlier_memory[:, None, :]
    carried = later_mask * (memory_outer * earlier_spatial)
    return spatial + carried + precision[:, :, None] * jnp.eye(NS, dtype=jnp.float32)


def draw_lower_blocks(key, part):
    spatial, memory = spatial_terms(key)
    return -(jnp.roll(memory, 1, axis=0)[:, :, None] * jnp.roll(spatial, 1, axis=0))


def draw_obs_prec(key, part):
    precision = obs_terms(key)
    return precision


def draw_prior_prec(key, part):
    key = jax.random.fold_in(key, 4)
    raw_values = jax.random.uniform(jax.random.fold_in(key, 1), (NF, NF), jnp.float32, -1.0, 1.0)
    identity = jnp.eye(NF, dtype=jnp.float32)
    symmetric = 0.5 * (raw_values + raw_values.T) * (0.5 / NF) * (1.0 - identity)
    spread = jnp.exp(jax.random.uniform(jax.random.fold_in(key, 2), (NF,), jnp.float32, math.log(0.5), math.log(2.0)))
    return symmetric + (1.0 + spread)[:, None] * identity


def block_levels(stream_key, extent, split, low, largest):
    factor_of, own = 1.0, jax.random.fold_in(stream_key, 6)
    for dim, shards_of in split:
        draws = jnp.exp(jax.random.uniform(jax.random.fold_in(own, dim), (shards_of,), jnp.float32, low / len(split), largest / len(split)))
        factor_of = factor_of * jnp.repeat(draws, extent[dim] // shards_of).reshape([-1 if axis == dim else 1 for axis in range(len(extent))])
    return factor_of


def centred(key, dims, scale, limit, shards=(), kind=jnp.bfloat16):
    values = jax.random.normal(key, dims, jnp.float32) * scale
    if len(shards) > 0:
        values = block_levels(key, dims, shards, -0.22, 0.18) * values
    return jnp.clip(values, min=-limit, max=limit).astype(kind)


def setup_inputs(seed: int = 0) -> dict:
    streams_of = jax.random.split(jax.random.key(seed), 6)
    return {
        "diag_blocks": draw_diag_blocks(jax.random.fold_in(streams_of[5], 71), 0),
        "lower_blocks": draw_lower_blocks(jax.random.fold_in(streams_of[5], 71), 0),
        "obs_prec": draw_obs_prec(jax.random.fold_in(streams_of[5], 71), 0),
        "covariates": centred(streams_of[3], (NT, NF, NS), (NT * NS) ** -0.5, 0.0234375, ((0, 32), (2, 8)), jnp.float32),
        "prior_prec": draw_prior_prec(jax.random.fold_in(streams_of[5], 71), 0),
    }


def outer_rows(left, right):
    return jnp.dot(left, right.T, precision=lax.Precision.HIGHEST)

def right_solve(factor, coupled):
    return lax.linalg.triangular_solve(factor, coupled, left_side=False, lower=True, transpose_a=True)

def eliminate(diag_part, lower_part, arrow_part, has_left):
    pivot_block = diag_part[0]
    upper_block = lower_part[0].T * has_left
    arrow_row = arrow_part[0]
    delta_diag = jnp.zeros_like(pivot_block)
    delta_arrow = jnp.zeros_like(arrow_row)
    tip_part = jnp.zeros((arrow_row.shape[0], arrow_row.shape[0]), jnp.float32)
    log_sum = jnp.zeros((), jnp.float32)
    factors = []
    coupling = jnp.zeros_like(pivot_block)
    for block_step in range(BLOCKS_DEV - 1):
        factor = jnp.linalg.cholesky(pivot_block)
        y_next = right_solve(factor, lower_part[block_step + 1])
        y_left = right_solve(factor, upper_block)
        y_arrow = right_solve(factor, arrow_row)
        coupling = -outer_rows(y_next, y_left)
        upper_block = -outer_rows(y_left, y_next)
        pivot_block = diag_part[block_step + 1] - outer_rows(y_next, y_next)
        arrow_row = arrow_part[block_step + 1] - outer_rows(y_arrow, y_next)
        delta_diag = delta_diag - outer_rows(y_left, y_left)
        delta_arrow = delta_arrow - outer_rows(y_arrow, y_left)
        tip_part = tip_part - outer_rows(y_arrow, y_arrow)
        log_sum = log_sum + jnp.sum(jnp.log(jnp.diagonal(factor)))
        factors.append(factor)
    return (jnp.stack(factors), pivot_block, coupling, arrow_row, delta_diag, delta_arrow, tip_part, log_sum)

def by_partition(values):
    return values.reshape((N_TM, BLOCKS_DEV) + values.shape[1:])

def reference(diag_blocks, lower_blocks, obs_prec, covariates, prior_prec):
    arrow_rows = covariates * obs_prec[:, None, :]
    tip_start = jnp.einsum('tfn,tgn->fg', arrow_rows, covariates, precision=lax.Precision.HIGHEST)
    has_left = (jnp.arange(N_TM) > 0).astype(jnp.float32)
    results = jax.vmap(eliminate)(by_partition(diag_blocks), by_partition(lower_blocks), by_partition(arrow_rows), has_left)
    factors, pivot_block, coupling, arrow_row, delta_diag, delta_arrow, tip_part, log_sum = results
    separator_diag = pivot_block + jnp.concatenate([delta_diag[1:], jnp.zeros_like(delta_diag[:1])], 0)
    separator_arrow = arrow_row + jnp.concatenate([delta_arrow[1:], jnp.zeros_like(delta_arrow[:1])], 0)
    interior_factors = factors.reshape((N_TM * (BLOCKS_DEV - 1), NS, NS))
    tip_block = prior_prec + (tip_start + jnp.sum(tip_part, 0))
    log_pivots = jnp.sum(log_sum) / (N_TM * (BLOCKS_DEV - 1) * NS)
    return (interior_factors, separator_diag, coupling, separator_arrow, tip_block, log_pivots)
```

```python
import functools

import jax
import jax.numpy as jnp
from jax import lax
from jax.experimental import pallas as pl
from jax.experimental.pallas import tpu as pltpu
from jax.sharding import PartitionSpec as P

B = 128
NB = 8
N = B * NB
NF = 64
PIECE = 6 * B
F32 = jnp.float32
BF16 = jnp.bfloat16
VMEM = pl.BlockSpec(memory_space=pltpu.VMEM)
SMEM = pl.BlockSpec(memory_space=pltpu.SMEM)
ANY = pl.BlockSpec(memory_space=pl.ANY)


def params():
    return pltpu.CompilerParams(vmem_limit_bytes=56 * 2**20)


def shape(*dims, dtype=F32):
    return jax.ShapeDtypeStruct(dims, dtype)


def split(x):
    high = x.astype(BF16)
    return high, (x - high.astype(F32)).astype(BF16)


def dot(a, b):
    return jnp.dot(a, b, preferred_element_type=F32)


def dot_t(a, b):
    return lax.dot_general(a, b, (((1,), (1,)), ((), ())), preferred_element_type=F32)


def dot3(ah, al, bh, bl):
    return dot(ah, bh) + (dot(ah, bl) + dot(al, bh))


def dot3_t(ah, al, bh, bl):
    return dot_t(ah, bh) + (dot_t(ah, bl) + dot_t(al, bh))


def block(index):
    return pl.ds(pl.multiple_of(index * B, B), B)


def sent_columns(row):
    chip = row // 2
    following = lax.rem(chip + 1, 4)
    across = lax.rem(row + 4, NB)
    flipped = across + 1 - 2 * lax.rem(across, 2)
    last = jnp.where(chip < 2, across, flipped)
    return [2 * chip, 2 * chip + 1, 2 * following, 2 * following + 1, last]


def pack_kernel(row_ref, diag_ref, obs_ref, cov_ref, piece_ref, arrows_ref, sem):
    copies = []
    for slot, column in enumerate(sent_columns(row_ref[0])):
        copy = pltpu.make_async_copy(
            diag_ref.at[0, :, block(column)], piece_ref.at[slot * B : (slot + 1) * B, :], sem.at[slot]
        )
        copy.start()
        copies.append(copy)
    tip = jnp.zeros((NF, NF), F32)
    for t in range(2):
        cov = cov_ref[t]
        arrow = cov * obs_ref[t : t + 1, :]
        arrows_ref[t] = arrow
        if t == 0:
            piece_ref[5 * B : 5 * B + NF, :] = arrow
        tip = tip + dot3_t(*split(arrow), *split(cov))
    piece_ref[5 * B + NF :, :] = jnp.concatenate([tip, jnp.zeros((NF, B - NF), F32)], axis=1)
    for copy in copies:
        copy.wait()


def diag_factor(S, between):
    lane = lax.broadcasted_iota(jnp.int32, (8, B), 1)
    sub = lax.broadcasted_iota(jnp.int32, (8, B), 0)
    n = B // 8
    Sv = [S[8 * v : 8 * v + 8, :] for v in range(n)]
    X, FD, SC = [], [], []

    def over_lanes(x, i):
        return jnp.broadcast_to(x[:, i : i + 1], (8, B))

    def over_rows(x, j):
        return jnp.broadcast_to(x[j : j + 1, :], (8, B))

    for g in range(n):
        base = 8 * g
        C = [over_lanes(Sv[g], base + i) for i in range(8)]
        Ct = {v: [over_lanes(Sv[v], base + i) for i in range(8)] for v in range(g + 1, n)}
        inside = (lane >= base) & (lane < base + 8)
        R = jnp.where(inside, (lane == base + sub).astype(F32), Sv[g])
        Rt = {v: jnp.where(inside, 0.0, Sv[v]) for v in range(g + 1, n)}
        scale = None
        fd = None
        for j in range(8):
            d = over_rows(C[j], j)
            r = 1.0 / d
            rs = lax.rsqrt(d)
            fc = C[j] * rs
            fd = fc if fd is None else jnp.where(lane == base + j, fc, fd)
            scale = rs if scale is None else jnp.where(sub == j, rs, scale)
            rowj = over_rows(R, j)
            cj = {i: over_rows(C[j], i) for i in range(j + 1, 8)}
            if j < 7:
                m = jnp.where(sub > j, C[j] * r, 0.0)
                R = R - m * rowj
                for i in range(j + 1, 8):
                    C[i] = C[i] - m * cj[i]
            for v in range(g + 1, n):
                mt = Ct[v][j] * r
                Rt[v] = Rt[v] - mt * rowj
                for i in range(j + 1, 8):
                    Ct[v][i] = Ct[v][i] - mt * cj[i]
        for v in range(g + 1, n):
            Sv[v] = Rt[v]
        X.append(R * scale)
        FD.append(jnp.where(inside & (lane <= base + sub), fd, 0.0))
        SC.append(scale)
        between(g)
    return X, FD, SC


def place_piece(source, slot_base, slots, row, D, sem, base):
    copies = []
    columns = sent_columns(row)
    for k in range(slots):
        slot = slot_base + k
        if slot < 5:
            copy = pltpu.make_async_copy(
                source.at[k * B : (k + 1) * B, :], D.at[block(row), block(columns[slot])], sem.at[base + k]
            )
            copy.start()
            copies.append(copy)
    return copies


def factor_kernel(
    where_ref, own, other, up, down, o_up, o_down, up2, down2, o_up2, o_down2, arrows_ref, lower_ref,
    f_ref, mh_ref, ml_ref, znh_ref, znl_ref, sa_ref, arrow_h_ref, arrow_l_ref, tip_ref,
    D, A, T, Fs, Fh, Fl, Uh, Ul, Mh, Ml, W, L1, sem, sem2,
):
    chip = where_ref[0]
    core = where_ref[1]
    row = 2 * chip + core

    def index(distance, same):
        c = lax.rem(chip + distance + 4, 4)
        return 2 * c + (core if same else 1 - core)

    sources = [
        (own, 0, 6, index(0, True)), (other, 0, 6, index(0, False)),
        (up, 0, 6, index(-1, True)), (down, 0, 6, index(1, True)),
        (o_up, 0, 6, index(-1, False)), (o_down, 0, 6, index(1, False)),
        (up2, 0, 3, index(2, True)), (down2, 3, 3, index(2, True)),
        (o_up2, 0, 3, index(2, False)), (o_down2, 3, 3, index(2, False)),
    ]
    copies = []
    count = 0
    for ref, first, slots, r in sources:
        copies += place_piece(ref, first, slots, r, D, sem, count)
        count += slots
        if first + slots == 6:
            tail = (slots - 1) * B
            copy = pltpu.make_async_copy(ref.at[tail : tail + NF, :], A.at[:, block(r)], sem2.at[count])
            copy.start()
            copies.append(copy)
            copy = pltpu.make_async_copy(ref.at[tail + NF : tail + B, :], T.at[r], sem2.at[count + 1])
            copy.start()
            copies.append(copy)
    last = pltpu.make_async_copy(lower_ref.at[1], L1, sem2.at[0])
    last.start()

    lane = lax.broadcasted_iota(jnp.int32, (8, B), 1)
    lane_b = lax.broadcasted_iota(jnp.int32, (B, B), 1)
    sub_b = lax.broadcasted_iota(jnp.int32, (B, B), 0)
    inverse_part = (lane_b // 8) <= (sub_b // 8)
    Fs[...] = jnp.zeros_like(Fs)
    Mh[...] = jnp.zeros_like(Mh)
    Ml[...] = jnp.zeros_like(Ml)
    acc = jnp.ones((8, B), F32)
    for copy in copies:
        copy.wait()
    for b in range(2, NB):
        if b // 2 == 3:
            for a in range(2):
                D[a * B : (a + 1) * B, b * B : (b + 1) * B] = D[b * B : (b + 1) * B, a * B : (a + 1) * B].T
        if b // 2 >= 2:
            a = ((b + 4) % NB) ^ 1
            D[a * B : (a + 1) * B, b * B : (b + 1) * B] = D[b * B : (b + 1) * B, a * B : (a + 1) * B].T
    W[0:B, :] = D[0:B, :]
    for J in range(NB):
        r0 = J * B
        r1 = r0 + B
        here = slice((J % 2) * B, (J % 2) * B + B)
        there = slice(((J + 1) % 2) * B, ((J + 1) % 2) * B + B)
        chunks = list(range(NB)) if J + 1 < NB else []

        def chunk(cb):
            cs = slice(cb * B, cb * B + B)
            rows = slice(r1, r1 + B)
            if cb >= J + 1:
                part = D[rows, cs]
                if J > 0:
                    part = part - dot3(Fh[rows, 0:r0], Fl[rows, 0:r0], Uh[0:r0, cs], Ul[0:r0, cs])
            elif cb < J:
                part = -dot3(Fh[rows, 0:r0], Fl[rows, 0:r0], Mh[0:r0, cs], Ml[0:r0, cs])
            else:
                part = jnp.zeros((B, B), F32)
            W[there, cs] = part

        def between(g):
            if chunks and g % 2 == 0:
                chunk(chunks.pop(0))

        X, FD, SC = diag_factor(W[here, r0:r1], between)
        while chunks:
            chunk(chunks.pop(0))
        for g in range(16):
            acc = jnp.where(lane == J * 16 + g, SC[g], acc)
        X = jnp.concatenate(X, 0)
        FD = jnp.concatenate(FD, 0)
        mjh, mjl = split(jnp.where(inverse_part, X, 0.0))
        Mh[r0:r1, r0:r1] = mjh
        Ml[r0:r1, r0:r1] = mjl
        Fs[r0:r1, r0:r1] = jnp.where(inverse_part, 0.0, X).T + FD
        if J > 0:
            wh, wl = split(dot3(mjh, mjl, *split(W[here, 0:r0])))
            Mh[r0:r1, 0:r0] = wh
            Ml[r0:r1, 0:r0] = wl
        if J + 1 < NB:
            w = dot3(mjh, mjl, *split(W[here, r1:]))
            wh, wl = split(w)
            Uh[r0:r1, r1:] = wh
            Ul[r0:r1, r1:] = wl
            f = w.T
            Fs[r1:, r0:r1] = f
            fh, fl = split(f)
            Fh[r1:, r0:r1] = fh
            Fl[r1:, r0:r1] = fl
            W[there, r1:] = W[there, r1:] - dot3(fh[0:B], fl[0:B], wh, wl)
            W[there, 0:r1] = W[there, 0:r1] - dot3(fh[0:B], fl[0:B], Mh[r0:r1, 0:r1], Ml[r0:r1, 0:r1])
    f_ref[0] = Fs[block(row), :]
    mh_ref[...] = Mh[...]
    ml_ref[...] = Ml[...]
    ah, al = split(A[...])
    arrow_h_ref[...] = ah
    arrow_l_ref[...] = al
    yh, yl = split(dot3_t(ah, al, Mh[...], Ml[...]))
    tip = -dot3_t(yh, yl, yh, yl)
    for r in range(NB):
        tip = tip + T[r, :, 0:NF]
    logs = jnp.broadcast_to(-jnp.sum(jnp.log(acc)), (8, NF))
    tip_ref[...] = jnp.concatenate([tip, logs], axis=0)
    last.wait()
    nh, nl = split(dot3_t(*split(L1[...]), Mh[...], Ml[...]))
    zh, zl = split(dot3(nh, nl, Mh[...], Ml[...]))
    znh_ref[...] = zh
    znl_ref[...] = zl
    sa_ref[0] = arrows_ref[1] - dot3_t(ah, al, zh, zl)


def factor_call(where, pieces, arrows, lower):
    return pl.pallas_call(
        factor_kernel,
        name="factor",
        out_shape=(
            shape(1, B, N), shape(N, N, dtype=BF16), shape(N, N, dtype=BF16), shape(B, N, dtype=BF16),
            shape(B, N, dtype=BF16), shape(1, NF, B), shape(NF, N, dtype=BF16), shape(NF, N, dtype=BF16),
            shape(NF + 8, NF),
        ),
        in_specs=[SMEM] + [ANY] * 10 + [VMEM, ANY],
        out_specs=(VMEM,) * 9,
        scratch_shapes=[
            pltpu.VMEM((N, N), F32), pltpu.VMEM((NF, N), F32), pltpu.VMEM((NB, NF, B), F32),
            pltpu.VMEM((N, N), F32),
        ]
        + [pltpu.VMEM((N, N), BF16)] * 6
        + [
            pltpu.VMEM((2 * B, N), F32), pltpu.VMEM((B, N), F32),
            pltpu.SemaphoreType.DMA((64,)), pltpu.SemaphoreType.DMA((64,)),
        ],
        compiler_params=params(),
        cost_estimate=pl.CostEstimate(flops=40 * 10**9, bytes_accessed=2 * 10**7, transcendentals=0),
    )(where, *pieces, arrows, lower)


def gather_rows(chip, core, refs, full, sem):
    def index(distance, same):
        c = lax.rem(chip + distance + 4, 4)
        return (2 * c + (core if same else 1 - core)) * B

    own, other, up, down, o_up, o_down, up2, down2, o_up2, o_down2 = refs
    half = B // 2
    parts = [
        (own, index(0, True), 0, B), (other, index(0, False), 0, B),
        (up, index(-1, True), 0, B), (down, index(1, True), 0, B),
        (o_up, index(-1, False), 0, B), (o_down, index(1, False), 0, B),
        (up2, index(2, True), 0, half), (down2, index(2, True), half, half),
        (o_up2, index(2, False), 0, half), (o_down2, index(2, False), half, half),
    ]
    copies = []
    for k, (ref, row, offset, size) in enumerate(parts):
        target = full.at[pl.ds(pl.multiple_of(row + offset, half), size), :]
        copy = pltpu.make_async_copy(ref, target, sem.at[k])
        copy.start()
        copies.append(copy)
    return copies


def handed_kernel(where_ref, *refs):
    pieces = refs[:10]
    mh_ref, ml_ref, ah_ref, al_ref, dd_ref, da_ref, lh_ref, ll_ref, L, sem = refs[10:]
    chip, core = where_ref[0], where_ref[1]
    copies = gather_rows(chip, core, pieces, L, sem)
    for copy in copies:
        copy.wait()
    keep = where_ref[2].astype(F32)
    left = L[:, block(2 * chip + core)].T * keep
    lh, ll = split(L[...] * keep)
    lh_ref[...] = lh
    ll_ref[...] = ll
    mh, ml = mh_ref[...], ml_ref[...]
    yh, yl = split(dot3_t(*split(left), mh, ml))
    zh, zl = split(dot3(yh, yl, mh, ml))
    dd_ref[...] = -dot3(zh, zl, lh, ll)
    da_ref[...] = -dot3_t(ah_ref[...], al_ref[...], zh, zl)


def handed_call(where, pieces, mh, ml, ah, al):
    return pl.pallas_call(
        handed_kernel,
        name="handed",
        out_shape=(shape(B, N), shape(NF, B), shape(N, N, dtype=BF16), shape(N, N, dtype=BF16)),
        in_specs=[SMEM] + [ANY] * 10 + [VMEM] * 4,
        out_specs=(VMEM,) * 4,
        scratch_shapes=[pltpu.VMEM((N, N), F32), pltpu.SemaphoreType.DMA((10,))],
        compiler_params=params(),
        cost_estimate=pl.CostEstimate(flops=4 * 10**9, bytes_accessed=10**7, transcendentals=0),
    )(where, *pieces, mh, ml, ah, al)


def coupling_kernel(zh_ref, zl_ref, lh_ref, ll_ref, out_ref):
    out_ref[0] = -dot3(zh_ref[...], zl_ref[...], lh_ref[...], ll_ref[...])


def coupling_call(zh, zl, lh, ll):
    return pl.pallas_call(
        coupling_kernel,
        name="coupling",
        out_shape=shape(1, B, N),
        in_specs=[VMEM] * 4,
        out_specs=VMEM,
        compiler_params=params(),
        cost_estimate=pl.CostEstimate(flops=10**9, bytes_accessed=5 * 10**6, transcendentals=0),
    )(zh, zl, lh, ll)


def next_kernel(where_ref, *refs):
    pieces = refs[:10]
    zh_ref, zl_ref, diag_ref, out_ref, L, D1, sem = refs[10:]
    copies = gather_rows(where_ref[0], where_ref[1], pieces, L, sem)
    copy = pltpu.make_async_copy(diag_ref.at[1], D1, sem.at[10])
    copy.start()
    for c in copies:
        c.wait()
    product = dot3_t(zh_ref[...], zl_ref[...], *split(L[...]))
    copy.wait()
    out_ref[...] = D1[...] - product


def next_call(where, pieces, zh, zl, diag):
    return pl.pallas_call(
        next_kernel,
        name="next",
        out_shape=shape(B, N),
        in_specs=[SMEM] + [ANY] * 10 + [VMEM] * 2 + [ANY],
        out_specs=VMEM,
        scratch_shapes=[pltpu.VMEM((N, N), F32), pltpu.VMEM((B, N), F32), pltpu.SemaphoreType.DMA((11,))],
        compiler_params=params(),
        cost_estimate=pl.CostEstimate(flops=2 * 10**9, bytes_accessed=8 * 10**6, transcendentals=0),
    )(where, *pieces, zh, zl, diag)


def pack_call(row, diag, obs, cov):
    return pl.pallas_call(
        pack_kernel,
        name="pack",
        out_shape=(shape(PIECE, B), shape(2, NF, B)),
        in_specs=[SMEM, ANY, VMEM, VMEM],
        out_specs=(VMEM, VMEM),
        scratch_shapes=[pltpu.SemaphoreType.DMA((5,))],
        compiler_params=params(),
    )(row, diag, obs, cov)


def ring(x):
    across = [(i, i ^ 1) for i in range(NB)]
    forth = [(i, (i + 2) % NB) for i in range(NB)]
    back = [(i, (i - 2) % NB) for i in range(NB)]
    send = functools.partial(lax.ppermute, axis_name="col")
    half = x.shape[0] // 2
    up = send(x, perm=forth)
    down = send(x, perm=back)
    other = send(x, perm=across)
    up2 = send(up[:half], perm=forth)
    down2 = send(down[half:], perm=back)
    o_up = send(up, perm=across)
    o_down = send(down, perm=across)
    o_up2 = send(up2, perm=across)
    o_down2 = send(down2, perm=across)
    return (x, other, up, down, o_up, o_down, up2, down2, o_up2, o_down2)


def butterfly(x, axis, moves):
    terms = [x] + [lax.ppermute(x, axis, [(i, i ^ k) for i in range(32)]) for k in moves]
    while len(terms) > 1:
        terms = [terms[k] + terms[k + 1] for k in range(0, len(terms), 2)]
    return terms[0]


def per_device(diag, lower, obs, cov, prior):
    col = lax.axis_index("col").astype(jnp.int32)
    tm = lax.axis_index("tm")
    where = jnp.stack([col // 2, col % 2, (tm > 0).astype(jnp.int32)])
    piece, arrows = pack_call(col[None], diag, obs, cov)
    pieces = ring(piece)
    left_pieces = ring(lower[0])
    next_pieces = ring(lower[1])
    factors, mh, ml, zh, zl, sep_arrow, ah, al, tip = factor_call(where, pieces, arrows, lower)
    delta_diag, delta_arrow, lh, ll = handed_call(where, left_pieces, mh, ml, ah, al)
    route = [(i, i - 1) for i in range(1, 32)]
    handed = [lax.ppermute(v, "tm", route) for v in (delta_diag, delta_arrow)]
    tip = butterfly(tip, "tm", range(1, 8))
    tip = butterfly(tip, "tm", range(8, 32, 8))
    coupling = coupling_call(zh, zl, lh, ll)
    pivot = next_call(where, next_pieces, zh, zl, diag)
    separator_diag = (pivot + handed[0])[None]
    separator_arrow = sep_arrow + handed[1][None]
    tip_block = prior + tip[:NF]
    log_pivots = tip[NF, 0] / (32 * N)
    return (factors, separator_diag, coupling, separator_arrow, tip_block, log_pivots)


def solution(mesh):
    return jax.shard_map(
        per_device,
        mesh=mesh,
        in_specs=(
            P("tm", "col", None),
            P("tm", "col", None),
            P("tm", "col"),
            P("tm", None, "col"),
            P(),
        ),
        out_specs=(
            P("tm", "col", None),
            P("tm", "col", None),
            P("tm", "col", None),
            P("tm", None, "col"),
            P(),
            P(),
        ),
        check_vma=False,
    )
```

```python
import functools

import jax
import jax.numpy as jnp
from jax import lax
from jax.experimental import pallas as pl
from jax.experimental.pallas import tpu as pltpu
from jax.sharding import PartitionSpec as P

B = 128
NB = 8
N = B * NB
NF = 64
PIECE = 6 * B
F32 = jnp.float32
BF16 = jnp.bfloat16
VMEM = pl.BlockSpec(memory_space=pltpu.VMEM)
SMEM = pl.BlockSpec(memory_space=pltpu.SMEM)
ANY = pl.BlockSpec(memory_space=pl.ANY)


def params():
    return pltpu.CompilerParams(vmem_limit_bytes=56 * 2**20)


def shape(*dims, dtype=F32):
    return jax.ShapeDtypeStruct(dims, dtype)


def split(x):
    high = x.astype(BF16)
    return high, (x - high.astype(F32)).astype(BF16)


def dot(a, b):
    return jnp.dot(a, b, preferred_element_type=F32)


def dot_t(a, b):
    return lax.dot_general(a, b, (((1,), (1,)), ((), ())), preferred_element_type=F32)


def stack(x):
    return jnp.concatenate(split(x), axis=0)


def dot3(a, bh, bl):
    rows = a.shape[0] // 2
    both = dot(a, bh)
    return both[:rows] + (both[rows:] + dot(a[:rows], bl))


def dot3_t(a, bh, bl):
    rows = a.shape[0] // 2
    both = dot_t(a, bh)
    return both[:rows] + (both[rows:] + dot_t(a[:rows], bl))


def block(index):
    return pl.ds(pl.multiple_of(index * B, B), B)


def sent_columns(row):
    chip = row // 2
    following = (chip + 1) % 4
    across = (row + 4) % NB
    flipped = across + 1 - 2 * (across % 2)
    last = across + (flipped - across) * (chip // 2)
    return [2 * chip, 2 * chip + 1, 2 * following, 2 * following + 1, last]


def pack_kernel(row_ref, diag_ref, obs_ref, cov_ref, piece_ref, arrows_ref, sem):
    copies = []
    for slot, column in enumerate(sent_columns(row_ref[0])):
        copy = pltpu.make_async_copy(
            diag_ref.at[0, :, block(column)], piece_ref.at[slot * B : (slot + 1) * B, :], sem.at[slot]
        )
        copy.start()
        copies.append(copy)
    tip = jnp.zeros((NF, NF), F32)
    for t in range(2):
        cov = cov_ref[t]
        arrow = cov * obs_ref[t : t + 1, :]
        arrows_ref[t] = arrow
        if t == 0:
            piece_ref[5 * B : 5 * B + NF, :] = arrow
        tip = tip + dot3_t(stack(arrow), *split(cov))
    piece_ref[5 * B + NF :, :] = jnp.concatenate([tip, jnp.zeros((NF, B - NF), F32)], axis=1)
    for copy in copies:
        copy.wait()


def diag_factor(S, between):
    lane = lax.broadcasted_iota(jnp.int32, (8, B), 1)
    sub = lax.broadcasted_iota(jnp.int32, (8, B), 0)
    n = B // 8
    Sv = [S[8 * v : 8 * v + 8, :] for v in range(n)]
    X, FD, SC = [], [], []

    def over_lanes(x, i):
        return jnp.broadcast_to(x[:, i : i + 1], (8, B))

    def over_rows(x, j):
        return jnp.broadcast_to(x[j : j + 1, :], (8, B))

    C = [over_lanes(Sv[0], i) for i in range(8)]
    for g in range(n):
        base = 8 * g
        Ct = {v: [over_lanes(Sv[v], base + i) for i in range(8)] for v in range(g + 1, n)}
        ahead = [over_lanes(Sv[g + 1], base + 8 + i) for i in range(8)] if g + 1 < n else None
        inside = (lane >= base) & (lane < base + 8)
        R = jnp.where(inside, (lane == base + sub).astype(F32), Sv[g])
        Rt = {v: jnp.where(inside, 0.0, Sv[v]) for v in range(g + 1, n)}
        scale = None
        fd = None
        for j in range(8):
            d = over_rows(C[j], j)
            r = 1.0 / d
            rs = lax.rsqrt(d)
            fc = C[j] * rs
            fd = fc if fd is None else jnp.where(lane == base + j, fc, fd)
            scale = rs if scale is None else jnp.where(sub == j, rs, scale)
            rowj = over_rows(R, j)
            cj = {i: over_rows(C[j], i) for i in range(j + 1, 8)}
            if j < 7:
                m = jnp.where(sub > j, C[j] * r, 0.0)
                R = R - m * rowj
                for i in range(j + 1, 8):
                    C[i] = C[i] - m * cj[i]
            for v in range(g + 1, n):
                mt = Ct[v][j] * r
                if v == g + 1:
                    for i in range(8):
                        ahead[i] = ahead[i] - mt * over_rows(Ct[v][j], i)
                Rt[v] = Rt[v] - mt * rowj
                for i in range(j + 1, 8):
                    Ct[v][i] = Ct[v][i] - mt * cj[i]
        for v in range(g + 1, n):
            Sv[v] = Rt[v]
        C = ahead
        X.append(R * scale)
        FD.append(jnp.where(inside & (lane <= base + sub), fd, 0.0))
        SC.append(scale)
        between(g)
    return X, FD, SC


def place_piece(source, slot_base, slots, row, D, sem, base):
    copies = []
    columns = sent_columns(row)
    for k in range(slots):
        slot = slot_base + k
        if slot < 5:
            copy = pltpu.make_async_copy(
                source.at[k * B : (k + 1) * B, :], D.at[block(row), block(columns[slot])], sem.at[base + k]
            )
            copy.start()
            copies.append(copy)
    return copies


def factor_kernel(
    where_ref, own, other, up, down, o_up, o_down, up2, down2, o_up2, o_down2,
    f_ref, mh_ref, ml_ref, arrow_ref, tip_ref,
    D, A, T, Fs, F2, Uh, Ul, Mh, Ml, W, sem, sem2, sem3,
):
    row = where_ref[0]
    chip = row // 2
    core = row % 2

    def index(distance, same):
        c = lax.rem(chip + distance + 4, 4)
        return 2 * c + (core if same else 1 - core)

    sources = [
        (own, 0, 6, index(0, True)), (other, 0, 6, index(0, False)),
        (up, 0, 6, index(-1, True)), (down, 0, 6, index(1, True)),
        (o_up, 0, 6, index(-1, False)), (o_down, 0, 6, index(1, False)),
        (up2, 0, 3, index(2, True)), (down2, 3, 3, index(2, True)),
        (o_up2, 0, 3, index(2, False)), (o_down2, 3, 3, index(2, False)),
    ]
    copies = []
    count = 0
    for ref, first, slots, r in sources:
        copies += place_piece(ref, first, slots, r, D, sem, count)
        count += slots
        if first + slots == 6:
            tail = (slots - 1) * B
            copy = pltpu.make_async_copy(ref.at[tail : tail + NF, :], A.at[:, block(r)], sem2.at[count])
            copy.start()
            copies.append(copy)
            copy = pltpu.make_async_copy(ref.at[tail + NF : tail + B, :], T.at[r], sem2.at[count + 1])
            copy.start()
            copies.append(copy)

    lane = lax.broadcasted_iota(jnp.int32, (8, B), 1)
    lane_b = lax.broadcasted_iota(jnp.int32, (B, B), 1)
    sub_b = lax.broadcasted_iota(jnp.int32, (B, B), 0)
    inverse_part = (lane_b // 8) <= (sub_b // 8)
    for b in range(0, NB, 2):
        corner = (slice(b * B, b * B + B), slice(b * B + B, b * B + 2 * B))
        Mh[corner] = jnp.zeros((B, B), BF16)
        Ml[corner] = jnp.zeros((B, B), BF16)
    acc = jnp.ones((8, B), F32)
    for copy in copies:
        copy.wait()
    for b in range(2, NB):
        if b // 2 == 3:
            for a in range(2):
                D[a * B : (a + 1) * B, b * B : (b + 1) * B] = D[b * B : (b + 1) * B, a * B : (a + 1) * B].T
        if b // 2 >= 2:
            a = ((b + 4) % NB) ^ 1
            D[a * B : (a + 1) * B, b * B : (b + 1) * B] = D[b * B : (b + 1) * B, a * B : (a + 1) * B].T
    W[0:B, :] = D[0:B, :]
    stores = []
    for J in range(NB):
        r0 = J * B
        r1 = r0 + B
        here = slice((J % 2) * B, (J % 2) * B + B)
        there = slice(((J + 1) % 2) * B, ((J + 1) % 2) * B + B)
        rows = slice(r1, r1 + B)
        coming = slice(2 * r1, 2 * r1 + 2 * B)
        chunks = []
        if J + 1 < NB:
            c = r1
            while c < N:
                e = min(N, c - c % 256 + 256)
                chunks.append((c, e))
                c = e
            c = 0
            while c < r0:
                chunks.append((c, min(r0, c + 256)))
                c += 256

        def chunk(c, e):
            cs = slice(c, e)
            if c >= r1:
                part = D[rows, cs]
                if J > 0:
                    part = part - dot3(F2[coming, 0:r0], Uh[0:r0, cs], Ul[0:r0, cs])
            else:
                part = -dot3(F2[coming, c:r0], Mh[c:r0, cs], Ml[c:r0, cs])
            W[there, cs] = part

        def between(g):
            if chunks and g % 2 == 0:
                chunk(*chunks.pop(0))

        X, FD, SC = diag_factor(W[here, r0:r1], between)
        while chunks:
            chunk(*chunks.pop(0))
        for g in range(16):
            acc = jnp.where(lane == J * 16 + g, SC[g], acc)
        X = jnp.concatenate(X, 0)
        FD = jnp.concatenate(FD, 0)
        inverse = jnp.where(inverse_part, X, 0.0)
        mjh, mjl = split(inverse)
        mj = jnp.concatenate([mjh, mjl], axis=0)
        Mh[r0:r1, r0:r1] = mjh
        Ml[r0:r1, r0:r1] = mjl
        if J + 1 < NB:
            w = dot3(mj, *split(W[here, r1:]))
            wh, wl = split(w)
            f = w.T
            next_f = stack(f[0:B])
            W[there, r1:] = W[there, r1:] - dot3(next_f, wh, wl)
            Uh[r0:r1, r1:] = wh
            Ul[r0:r1, r1:] = wl
            Fs[r1:, r0:r1] = f
            fh, fl = split(f)
            for K in range(J + 1, NB):
                o = K * B - r1
                F2[2 * K * B : 2 * K * B + B, r0:r1] = fh[o : o + B]
                F2[2 * K * B + B : 2 * K * B + 2 * B, r0:r1] = fl[o : o + B]
        if J > 0:
            wh, wl = split(dot3(mj, *split(W[here, 0:r0])))
            Mh[r0:r1, 0:r0] = wh
            Ml[r0:r1, 0:r0] = wl
        if J + 1 < NB:
            if J > 0:
                W[there, 0:r0] = W[there, 0:r0] - dot3(next_f, wh, wl)
            W[there, r0:r1] = -dot3(next_f, mjh, mjl)
        Fs[r0:r1, r0:r1] = jnp.where(inverse_part, 0.0, X).T + FD
        width = r1 + B * ((J + 1) % 2)
        for k, (source, target) in enumerate(((Mh, mh_ref), (Ml, ml_ref))):
            copy = pltpu.make_async_copy(
                source.at[r0:r1, 0:width], target.at[r0:r1, 0:width], sem3.at[2 * J + k]
            )
            copy.start()
            stores.append(copy)
    a2 = stack(A[...])
    arrow_ref[...] = a2
    tip = jnp.zeros((NF, NF), F32)
    for j in range(0, N, 256):
        y = dot3_t(a2[:, 0 : j + 256], Mh[j : j + 256, 0 : j + 256], Ml[j : j + 256, 0 : j + 256])
        tip = tip - dot3_t(stack(y), *split(y))
    for r in range(NB):
        tip = tip + T[r, :, 0:NF]
    logs = jnp.broadcast_to(-jnp.sum(jnp.log(acc)), (8, NF))
    tip_ref[...] = jnp.concatenate([tip, logs], axis=0)
    for b in range(NB):
        cs = slice(b * B, b * B + B)
        f_ref[0, :, cs] = jnp.where(b <= row, Fs[block(row), cs], 0.0)
    for copy in stores:
        copy.wait()


def factor_call(where, pieces):
    return pl.pallas_call(
        factor_kernel,
        name="factor",
        out_shape=(
            shape(1, B, N), shape(N, N, dtype=BF16), shape(N, N, dtype=BF16),
            shape(2 * NF, N, dtype=BF16), shape(NF + 8, NF),
        ),
        in_specs=[SMEM] + [ANY] * 10,
        out_specs=(VMEM, ANY, ANY, VMEM, VMEM),
        scratch_shapes=[
            pltpu.VMEM((N, N), F32), pltpu.VMEM((NF, N), F32), pltpu.VMEM((NB, NF, B), F32),
            pltpu.VMEM((N, N), F32), pltpu.VMEM((2 * N, N), BF16),
        ]
        + [pltpu.VMEM((N, N), BF16)] * 4
        + [
            pltpu.VMEM((2 * B, N), F32),
            pltpu.SemaphoreType.DMA((64,)), pltpu.SemaphoreType.DMA((64,)), pltpu.SemaphoreType.DMA((16,)),
        ],
        compiler_params=params(),
        cost_estimate=pl.CostEstimate(flops=40 * 10**9, bytes_accessed=2 * 10**7, transcendentals=0),
    )(where, *pieces)


def fetch_inverse(mh_ref, ml_ref, Mh, Ml, sem):
    copies = []
    for j in range(4):
        area = (slice(j * 256, j * 256 + 256), slice(0, j * 256 + 256))
        for k, (source, target) in enumerate(((mh_ref, Mh), (ml_ref, Ml))):
            copy = pltpu.make_async_copy(source.at[area], target.at[area], sem.at[2 * j + k])
            copy.start()
            copies.append(copy)
    return copies


def solved(rows, Mh, Ml):
    a = stack(rows)
    y = [
        stack(dot3_t(a[:, 0 : j + 256], Mh[j : j + 256, 0 : j + 256], Ml[j : j + 256, 0 : j + 256]))
        for j in range(0, N, 256)
    ]
    y = jnp.concatenate(y, axis=1)
    z = [
        stack(dot3(y[:, k:], Mh[k:, k : k + 256], Ml[k:, k : k + 256])) for k in range(0, N, 256)
    ]
    return jnp.concatenate(z, axis=1)


def handed_kernel(where_ref, both_ref, mh_ref, ml_ref, arrow_ref, dd_ref, da_ref, C, L, Mh, Ml, sem):
    columns = pltpu.make_async_copy(both_ref.at[0, :, block(where_ref[0])], C, sem.at[8])
    columns.start()
    copies = fetch_inverse(mh_ref, ml_ref, Mh, Ml, sem)
    whole = pltpu.make_async_copy(both_ref.at[0], L, sem.at[9])
    whole.start()
    columns.wait()
    keep = where_ref[1].astype(F32)
    left = C[...].T * keep
    for copy in copies:
        copy.wait()
    z = solved(left, Mh, Ml)
    da_ref[...] = -dot3_t(arrow_ref[...], z[:B], z[B:])
    whole.wait()
    for c in range(0, N, 256):
        dd_ref[:, c : c + 256] = -dot3(z, *split(L[:, c : c + 256] * keep))


def handed_call(where, both, mh, ml, arrow):
    return pl.pallas_call(
        handed_kernel,
        name="handed",
        out_shape=(shape(B, N), shape(NF, B)),
        in_specs=[SMEM, ANY, ANY, ANY, VMEM],
        out_specs=(VMEM, VMEM),
        scratch_shapes=[
            pltpu.VMEM((N, B), F32), pltpu.VMEM((N, N), F32), pltpu.VMEM((N, N), BF16),
            pltpu.VMEM((N, N), BF16), pltpu.SemaphoreType.DMA((10,)),
        ],
        compiler_params=params(),
        cost_estimate=pl.CostEstimate(flops=4 * 10**9, bytes_accessed=10**7, transcendentals=0),
    )(where, both, mh, ml, arrow)


def rest_kernel(
    where_ref, both_ref, lower_ref, diag_ref, mh_ref, ml_ref, arrow_ref, arrows_ref,
    out_ref, pivot_ref, sa_ref, L0, L1, own, D1, Mh, Ml, sem,
):
    own_copy = pltpu.make_async_copy(lower_ref.at[1], own, sem.at[8])
    own_copy.start()
    copies = fetch_inverse(mh_ref, ml_ref, Mh, Ml, sem)
    left_copy = pltpu.make_async_copy(both_ref.at[0], L0, sem.at[9])
    left_copy.start()
    next_copy = pltpu.make_async_copy(both_ref.at[1], L1, sem.at[10])
    next_copy.start()
    diag_copy = pltpu.make_async_copy(diag_ref.at[1], D1, sem.at[11])
    diag_copy.start()
    own_copy.wait()
    for copy in copies:
        copy.wait()
    keep = where_ref[1].astype(F32)
    z = solved(own[...], Mh, Ml)
    sa_ref[0] = arrows_ref[1] - dot3_t(arrow_ref[...], z[:B], z[B:])
    left_copy.wait()
    for c in range(0, N, 256):
        out_ref[0, :, c : c + 256] = -dot3(z, *split(L0[:, c : c + 256] * keep))
    next_copy.wait()
    diag_copy.wait()
    for c in range(0, N, 256):
        pivot_ref[:, c : c + 256] = D1[:, c : c + 256] - dot3_t(z, *split(L1[c : c + 256, :]))


def rest_call(where, both, lower, diag, mh, ml, arrow, arrows):
    return pl.pallas_call(
        rest_kernel,
        name="rest",
        out_shape=(shape(1, B, N), shape(B, N), shape(1, NF, B)),
        in_specs=[SMEM] + [ANY] * 5 + [VMEM] * 2,
        out_specs=(VMEM,) * 3,
        scratch_shapes=[
            pltpu.VMEM((N, N), F32), pltpu.VMEM((N, N), F32), pltpu.VMEM((B, N), F32),
            pltpu.VMEM((B, N), F32), pltpu.VMEM((N, N), BF16), pltpu.VMEM((N, N), BF16),
            pltpu.SemaphoreType.DMA((12,)),
        ],
        compiler_params=params(),
        cost_estimate=pl.CostEstimate(flops=6 * 10**9, bytes_accessed=15 * 10**6, transcendentals=0),
    )(where, both, lower, diag, mh, ml, arrow, arrows)


def pack_call(row, diag, obs, cov):
    return pl.pallas_call(
        pack_kernel,
        name="pack",
        out_shape=(shape(PIECE, B), shape(2, NF, B)),
        in_specs=[SMEM, ANY, VMEM, VMEM],
        out_specs=(VMEM, VMEM),
        scratch_shapes=[pltpu.SemaphoreType.DMA((5,))],
        compiler_params=params(),
    )(row, diag, obs, cov)


def ring(x):
    across = [(i, i ^ 1) for i in range(NB)]
    forth = [(i, (i + 2) % NB) for i in range(NB)]
    back = [(i, (i - 2) % NB) for i in range(NB)]
    send = functools.partial(lax.ppermute, axis_name="col")
    half = x.shape[0] // 2
    up = send(x, perm=forth)
    down = send(x, perm=back)
    other = send(x, perm=across)
    up2 = send(up[:half], perm=forth)
    down2 = send(down[half:], perm=back)
    o_up = send(up, perm=across)
    o_down = send(down, perm=across)
    o_up2 = send(up2, perm=across)
    o_down2 = send(down2, perm=across)
    return (x, other, up, down, o_up, o_down, up2, down2, o_up2, o_down2)


def butterfly(x, axis, steps):
    for k in steps:
        x = x + lax.ppermute(x, axis, [(i, i ^ k) for i in range(32)])
    return x


def per_device(diag, lower, obs, cov, prior):
    col = lax.axis_index("col").astype(jnp.int32)
    tm = lax.axis_index("tm")
    where = jnp.stack([col, (tm > 0).astype(jnp.int32)])
    both = lax.all_gather(lower, "col", axis=1, tiled=True)
    piece, arrows = pack_call(col[None], diag, obs, cov)
    pieces = ring(piece)
    factors, mh, ml, arrow, tip = factor_call(where, pieces)
    delta = handed_call(where, both, mh, ml, arrow)
    route = [(i, i - 1) for i in range(1, 32)]
    handed = [lax.ppermute(v, "tm", route) for v in delta]
    coupling, pivot, sep_arrow = rest_call(where, both, lower, diag, mh, ml, arrow, arrows)
    tip, delta = lax.optimization_barrier((tip, delta))
    tip = butterfly(tip, "tm", (1, 2, 4, 8, 16))
    separator_diag = (pivot + handed[0])[None]
    separator_arrow = sep_arrow + handed[1][None]
    tip_block = prior + tip[:NF]
    log_pivots = tip[NF, 0] / (32 * N)
    return (factors, separator_diag, coupling, separator_arrow, tip_block, log_pivots)


def solution(mesh):
    return jax.shard_map(
        per_device,
        mesh=mesh,
        in_specs=(
            P("tm", "col", None),
            P("tm", "col", None),
            P("tm", "col"),
            P("tm", None, "col"),
            P(),
        ),
        out_specs=(
            P("tm", "col", None),
            P("tm", "col", None),
            P("tm", "col", None),
            P("tm", None, "col"),
            P(),
            P(),
        ),
        check_vma=False,
    )
```

```python
import functools

import jax
import jax.numpy as jnp
from jax import lax
from jax.experimental import pallas as pl
from jax.experimental.pallas import tpu as pltpu
from jax.sharding import PartitionSpec as P

B = 128
NB = 8
N = B * NB
NF = 64
PIECE = 6 * B
F32 = jnp.float32
BF16 = jnp.bfloat16
VMEM = pl.BlockSpec(memory_space=pltpu.VMEM)
SMEM = pl.BlockSpec(memory_space=pltpu.SMEM)
ANY = pl.BlockSpec(memory_space=pl.ANY)


def params():
    return pltpu.CompilerParams(vmem_limit_bytes=56 * 2**20)


def shape(*dims, dtype=F32):
    return jax.ShapeDtypeStruct(dims, dtype)


def split(x):
    high = x.astype(BF16)
    return high, (x - high.astype(F32)).astype(BF16)


def dot(a, b):
    return jnp.dot(a, b, preferred_element_type=F32)


def dot_t(a, b):
    return lax.dot_general(a, b, (((1,), (1,)), ((), ())), preferred_element_type=F32)


def stack(x):
    return jnp.concatenate(split(x), axis=0)


def dot3(a, bh, bl):
    rows = a.shape[0] // 2
    both = dot(a, bh)
    return both[:rows] + (both[rows:] + dot(a[:rows], bl))


def dot3_t(a, bh, bl):
    rows = a.shape[0] // 2
    both = dot_t(a, bh)
    return both[:rows] + (both[rows:] + dot_t(a[:rows], bl))


def block(index):
    return pl.ds(pl.multiple_of(index * B, B), B)


def sent_columns(row):
    chip = row // 2
    following = (chip + 1) % 4
    across = (row + 4) % NB
    flipped = across + 1 - 2 * (across % 2)
    last = across + (flipped - across) * (chip // 2)
    return [2 * chip, 2 * chip + 1, 2 * following, 2 * following + 1, last]


def pack_kernel(row_ref, diag_ref, obs_ref, cov_ref, piece_ref, arrows_ref, sem):
    copies = []
    for slot, column in enumerate(sent_columns(row_ref[0])):
        copy = pltpu.make_async_copy(
            diag_ref.at[0, :, block(column)], piece_ref.at[slot * B : (slot + 1) * B, :], sem.at[slot]
        )
        copy.start()
        copies.append(copy)
    tip = jnp.zeros((NF, NF), F32)
    for t in range(2):
        cov = cov_ref[t]
        arrow = cov * obs_ref[t : t + 1, :]
        arrows_ref[t] = arrow
        if t == 0:
            piece_ref[5 * B : 5 * B + NF, :] = arrow
        tip = tip + dot3_t(stack(arrow), *split(cov))
    piece_ref[5 * B + NF :, :] = jnp.concatenate([tip, jnp.zeros((NF, B - NF), F32)], axis=1)
    for copy in copies:
        copy.wait()


def diag_factor(S, between):
    lane = lax.broadcasted_iota(jnp.int32, (8, B), 1)
    sub = lax.broadcasted_iota(jnp.int32, (8, B), 0)
    H = B // 2
    Sv = [S[8 * v : 8 * v + 8, :] for v in range(B // 8)]
    X, FD, SC = [], [], []

    def over_lanes(x, i):
        return jnp.broadcast_to(x[:, i : i + 1], (8, B))

    def over_rows(x, j):
        return jnp.broadcast_to(x[j : j + 1, :], (8, B))

    for g in range(B // 8):
        base = 8 * g
        end = 8 if g < 8 else 16
        if g == 8:
            top = jnp.concatenate(X, axis=0)
            lane_h = lax.broadcasted_iota(jnp.int32, (H, B), 1)
            sub_h = lax.broadcasted_iota(jnp.int32, (H, B), 0)
            kept = jnp.where((lane_h >= H) | (lane_h // 8 <= sub_h // 8), top, 0.0)
            kh, kl = split(kept)
            fh, fl = split(top[:, H:].T)
            product = dot(jnp.concatenate([fh, fl, fh], axis=1), jnp.concatenate([kh, kh, kl], axis=0))
            for v in range(8, 16):
                rows = product[8 * v - H : 8 * v - H + 8, :]
                Sv[v] = jnp.where(lane >= H, Sv[v], 0.0) - rows
        if g % 8 == 0:
            C = [over_lanes(Sv[g], base + i) for i in range(8)]
        Ct = {v: [over_lanes(Sv[v], base + i) for i in range(8)] for v in range(g + 1, end) if v > g + 1 or g % 8 == 0}
        if g % 8 > 0 and g + 1 < end:
            Ct[g + 1] = second
        second = [over_lanes(Sv[g + 2], base + 8 + i) for i in range(8)] if g + 2 < end else None
        ahead = [over_lanes(Sv[g + 1], base + 8 + i) for i in range(8)] if g + 1 < end else None
        inside = (lane >= base) & (lane < base + 8)
        R = jnp.where(inside, (lane == base + sub).astype(F32), Sv[g])
        Rt = {v: jnp.where(inside, 0.0, Sv[v]) for v in range(g + 1, end)}
        scale = None
        fd = None
        rj, rows = [], []
        for j in range(8):
            d = over_rows(C[j], j)
            r = 1.0 / d
            rs = lax.rsqrt(d)
            fc = C[j] * rs
            fd = fc if fd is None else jnp.where(lane == base + j, fc, fd)
            scale = rs if scale is None else jnp.where(sub == j, rs, scale)
            rj.append(r)
            rows.append(over_rows(R, j))
            if j < 7:
                m = jnp.where(sub > j, C[j] * r, 0.0)
                R = R - m * rows[j]
                for i in range(j + 1, 8):
                    C[i] = C[i] - m * over_rows(C[j], i)
        for v in range(g + 1, end):
            for j in range(8):
                mt = Ct[v][j] * rj[j]
                if v == g + 1:
                    for i in range(8):
                        ahead[i] = ahead[i] - mt * over_rows(Ct[v][j], i)
                if v == g + 2:
                    for i in range(8):
                        second[i] = second[i] - mt * over_rows(Ct[g + 1][j], i)
                Rt[v] = Rt[v] - mt * rows[j]
                for i in range(j + 1, 8):
                    Ct[v][i] = Ct[v][i] - mt * over_rows(C[j], i)
        for v in range(g + 1, end):
            Sv[v] = Rt[v]
        C = ahead
        X.append(R * scale)
        FD.append(jnp.where(inside & (lane <= base + sub), fd, 0.0))
        SC.append(scale)
        between(g)
    return X, FD, SC


def place_piece(source, slot_base, slots, row, D, sem, base):
    copies = []
    columns = sent_columns(row)
    for k in range(slots):
        slot = slot_base + k
        if slot < 5:
            copy = pltpu.make_async_copy(
                source.at[k * B : (k + 1) * B, :], D.at[block(row), block(columns[slot])], sem.at[base + k]
            )
            copy.start()
            copies.append(copy)
    return copies


def factor_kernel(
    where_ref, own, other, up, down, o_up, o_down, up2, down2, o_up2, o_down2, lower_ref,
    f_ref, mh_ref, ml_ref, arrow_ref, z_ref, tip_ref,
    D, A, T, Fs, F2, Uh, Ul, Mh, Ml, W, P, L1, G, Z, sem, sem2, sem3,
):
    row = where_ref[0]
    chip = row // 2
    core = row % 2

    def index(distance, same):
        c = lax.rem(chip + distance + 4, 4)
        return 2 * c + (core if same else 1 - core)

    sources = [
        (own, 0, 6, index(0, True)), (other, 0, 6, index(0, False)),
        (up, 0, 6, index(-1, True)), (down, 0, 6, index(1, True)),
        (o_up, 0, 6, index(-1, False)), (o_down, 0, 6, index(1, False)),
        (up2, 0, 3, index(2, True)), (down2, 3, 3, index(2, True)),
        (o_up2, 0, 3, index(2, False)), (o_down2, 3, 3, index(2, False)),
    ]
    copies = []
    count = 0
    for ref, first, slots, r in sources:
        copies += place_piece(ref, first, slots, r, D, sem, count)
        count += slots
        if first + slots == 6:
            tail = (slots - 1) * B
            copy = pltpu.make_async_copy(ref.at[tail : tail + NF, :], A.at[:, block(r)], sem2.at[count])
            copy.start()
            copies.append(copy)
            copy = pltpu.make_async_copy(ref.at[tail + NF : tail + B, :], T.at[r], sem2.at[count + 1])
            copy.start()
            copies.append(copy)

    copy = pltpu.make_async_copy(lower_ref.at[1], L1, sem2.at[0])
    copy.start()
    copies.append(copy)

    lane = lax.broadcasted_iota(jnp.int32, (8, B), 1)
    lane_b = lax.broadcasted_iota(jnp.int32, (B, B), 1)
    sub_b = lax.broadcasted_iota(jnp.int32, (B, B), 0)
    inverse_part = (lane_b // 8) <= (sub_b // 8)
    for b in range(0, NB, 2):
        corner = (slice(b * B, b * B + B), slice(b * B + B, b * B + 2 * B))
        Mh[corner] = jnp.zeros((B, B), BF16)
        Ml[corner] = jnp.zeros((B, B), BF16)
    acc = jnp.ones((8, B), F32)
    for copy in copies:
        copy.wait()
    for b in range(2, NB):
        if b // 2 == 3:
            for a in range(2):
                D[a * B : (a + 1) * B, b * B : (b + 1) * B] = D[b * B : (b + 1) * B, a * B : (a + 1) * B].T
        if b // 2 >= 2:
            a = ((b + 4) % NB) ^ 1
            D[a * B : (a + 1) * B, b * B : (b + 1) * B] = D[b * B : (b + 1) * B, a * B : (a + 1) * B].T
    W[0:B, :] = D[0:B, :]
    stores = []
    tips = [sum(T[r, :, 0:NF] for r in range(NB))]
    S = D[0:B, 0:B]

    def split_rows():
        a2 = stack(A[...])
        arrow_ref[...] = a2
        nh, nl = split(L1[...])
        G[0:B, :] = nh
        G[B : B + NF, :] = a2[0:NF]
        G[B + NF : 2 * B + NF, :] = nl
        G[2 * B + NF :, :] = a2[NF:]
        Z[...] = jnp.zeros_like(Z)

    deferred = [split_rows]
    for J in range(NB):
        r0 = J * B
        r1 = r0 + B
        r2 = r1 + B
        here = slice((J % 2) * B, (J % 2) * B + B)
        there = slice(((J + 1) % 2) * B, ((J + 1) % 2) * B + B)
        per_group = -(-len(deferred) // 14)

        def between(g):
            for work in deferred[:per_group]:
                work()
            del deferred[:per_group]

        X, FD, SC = diag_factor(S, between)
        for g in range(16):
            acc = jnp.where(lane == J * 16 + g, SC[g], acc)
        X = jnp.concatenate(X, 0)
        FD = jnp.concatenate(FD, 0)
        mjh, mjl = split(jnp.where(inverse_part, X, 0.0))
        mj = jnp.concatenate([mjh, mjl], axis=0)
        Mh[r0:r1, r0:r1] = mjh
        Ml[r0:r1, r0:r1] = mjl
        Fs[r0:r1, r0:r1] = jnp.where(inverse_part, 0.0, X).T + FD

        def keep_columns(w, c, r0=r0, r1=r1):
            wh, wl = split(w)
            e = c + w.shape[1]
            Uh[r0:r1, c:e] = wh
            Ul[r0:r1, c:e] = wl
            f = w.T
            Fs[c:e, r0:r1] = f
            fh, fl = split(f)
            for K in range(c // B, e // B):
                o = K * B - c
                F2[2 * K * B : 2 * K * B + B, r0:r1] = fh[o : o + B]
                F2[2 * K * B + B : 2 * K * B + 2 * B, r0:r1] = fl[o : o + B]
            return jnp.concatenate([fh[0:B], fl[0:B]], axis=0), wh, wl

        def columns(c, e, J=J, here=here, mj=mj, keep_columns=keep_columns):
            keep_columns(dot3(mj, *split(W[here, c:e])), c)

        def inverse_row(c, e, r0=r0, r1=r1, here=here, mj=mj):
            wh, wl = split(dot3(mj, *split(W[here, c:e])))
            Mh[r0:r1, c:e] = wh
            Ml[r0:r1, c:e] = wl

        def store_row(J=J, r0=r0, r1=r1):
            width = r1 + B * ((J + 1) % 2)
            for k, (source, target) in enumerate(((Mh, mh_ref), (Ml, ml_ref))):
                copy = pltpu.make_async_copy(
                    source.at[r0:r1, 0:width], target.at[r0:r1, 0:width], sem3.at[2 * J + k]
                )
                copy.start()
                stores.append(copy)

        def solve_rows(r1=r1):
            pair = slice(r1 - 2 * B, r1)
            y = dot3_t(G[:, 0:r1], Mh[pair, 0:r1], Ml[pair, 0:r1])
            arrow = y[B:]
            tips.append(-dot3_t(stack(arrow), *split(arrow)))
            Z[:, 0:r1] = Z[:, 0:r1] + dot3(stack(y[0:B]), Mh[pair, 0:r1], Ml[pair, 0:r1])

        def next_row(c, e, r1=r1, r2=r2, there=there):
            coming = slice(2 * r1, 2 * r2)
            if c >= r1:
                W[there, c:e] = D[r1:r2, c:e] - dot3(F2[coming, 0:r1], Uh[0:r1, c:e], Ul[0:r1, c:e])
            else:
                W[there, c:e] = -dot3(F2[coming, c:r1], Mh[c:r1, c:e], Ml[c:r1, c:e])

        def pieces_of(c, e):
            while c < e:
                stop = min(e, c - c % 256 + 256)
                yield c, stop
                c = stop

        def partial_pivot(r1=r1, r2=r2, J=J):
            P[...] = D[r2 : r2 + B, r2 : r2 + B] - dot3(
                F2[2 * r2 : 2 * r2 + 2 * B, 0:r1], Uh[0:r1, r2 : r2 + B], Ul[0:r1, r2 : r2 + B]
            )

        if J + 1 < NB:
            f2, wh, wl = keep_columns(dot3(mj, *split(W[here, r1:r2])), r1)
            base = P[...] if J > 0 else D[r1:r2, r1:r2]
            S = base - dot3(f2, wh, wl)
        for c, e in pieces_of(r2, N):
            deferred.append(functools.partial(columns, c, e))
        if J + 2 < NB:
            deferred.append(partial_pivot)
            for c, e in pieces_of(r2, N):
                deferred.append(functools.partial(next_row, c, e))
        for c, e in pieces_of(0, r0):
            deferred.append(functools.partial(inverse_row, c, e))
        deferred.append(store_row)
        if J % 2 == 1:
            solves = [solve_rows]
        else:
            solves = []
        if J + 1 < NB:
            for c, e in pieces_of(0, r1):
                deferred.append(functools.partial(next_row, c, e))
        deferred += solves
    for work in deferred:
        work()
    z_ref[...] = stack(Z[...])
    tip = sum(tips)
    logs = jnp.broadcast_to(-jnp.sum(jnp.log(acc)), (8, NF))
    tip_ref[...] = jnp.concatenate([tip, logs], axis=0)
    for b in range(NB):
        cs = slice(b * B, b * B + B)
        f_ref[0, :, cs] = jnp.where(b <= row, Fs[block(row), cs], 0.0)
    for copy in stores:
        copy.wait()


def factor_call(where, pieces, lower):
    return pl.pallas_call(
        factor_kernel,
        name="factor",
        out_shape=(
            shape(1, B, N), shape(N, N, dtype=BF16), shape(N, N, dtype=BF16),
            shape(2 * NF, N, dtype=BF16), shape(2 * B, N, dtype=BF16), shape(NF + 8, NF),
        ),
        in_specs=[SMEM] + [ANY] * 11,
        out_specs=(VMEM, ANY, ANY, VMEM, VMEM, VMEM),
        scratch_shapes=[
            pltpu.VMEM((N, N), F32), pltpu.VMEM((NF, N), F32), pltpu.VMEM((NB, NF, B), F32),
            pltpu.VMEM((N, N), F32), pltpu.VMEM((2 * N, N), BF16),
        ]
        + [pltpu.VMEM((N, N), BF16)] * 4
        + [
            pltpu.VMEM((2 * B, N), F32), pltpu.VMEM((B, B), F32), pltpu.VMEM((B, N), F32),
            pltpu.VMEM((2 * B + 2 * NF, N), BF16), pltpu.VMEM((B, N), F32),
            pltpu.SemaphoreType.DMA((64,)), pltpu.SemaphoreType.DMA((64,)), pltpu.SemaphoreType.DMA((16,)),
        ],
        compiler_params=params(),
        cost_estimate=pl.CostEstimate(flops=40 * 10**9, bytes_accessed=2 * 10**7, transcendentals=0),
    )(where, *pieces, lower)


def fetch_inverse(mh_ref, ml_ref, Mh, Ml, sem):
    copies = []
    for j in range(4):
        area = (slice(j * 256, j * 256 + 256), slice(0, j * 256 + 256))
        for k, (source, target) in enumerate(((mh_ref, Mh), (ml_ref, Ml))):
            copy = pltpu.make_async_copy(source.at[area], target.at[area], sem.at[2 * j + k])
            copy.start()
            copies.append(copy)
    return copies


def solved(rows, Mh, Ml, copies):
    a = stack(rows)
    y = []
    for k, j in enumerate(range(0, N, 256)):
        copies[2 * k].wait()
        copies[2 * k + 1].wait()
        y.append(stack(dot3_t(a[:, 0 : j + 256], Mh[j : j + 256, 0 : j + 256], Ml[j : j + 256, 0 : j + 256])))
    y = jnp.concatenate(y, axis=1)
    z = [
        stack(dot3(y[:, k:], Mh[k:, k : k + 256], Ml[k:, k : k + 256])) for k in range(0, N, 256)
    ]
    return jnp.concatenate(z, axis=1)


def handed_kernel(where_ref, both_ref, mh_ref, ml_ref, arrow_ref, out_ref, C, L, Mh, Ml, sem):
    columns = pltpu.make_async_copy(both_ref.at[0, :, block(where_ref[0])], C, sem.at[8])
    columns.start()
    copies = fetch_inverse(mh_ref, ml_ref, Mh, Ml, sem)
    whole = pltpu.make_async_copy(both_ref.at[0], L, sem.at[9])
    whole.start()
    columns.wait()
    z = solved(C[...].T, Mh, Ml, copies)
    arrow = -dot3_t(arrow_ref[...], z[:B], z[B:])
    for k in range(NF // 8):
        out_ref[B:, k * B : (k + 1) * B] = arrow[8 * k : 8 * k + 8, :]
    whole.wait()
    for c in range(0, N, 256):
        out_ref[0:B, c : c + 256] = -dot3(z, *split(L[:, c : c + 256]))


def handed_call(where, both, mh, ml, arrow):
    return pl.pallas_call(
        handed_kernel,
        name="handed",
        out_shape=shape(B + 8, N),
        in_specs=[SMEM, ANY, ANY, ANY, VMEM],
        out_specs=VMEM,
        scratch_shapes=[
            pltpu.VMEM((N, B), F32), pltpu.VMEM((N, N), F32), pltpu.VMEM((N, N), BF16),
            pltpu.VMEM((N, N), BF16), pltpu.SemaphoreType.DMA((10,)),
        ],
        compiler_params=params(),
        cost_estimate=pl.CostEstimate(flops=4 * 10**9, bytes_accessed=10**7, transcendentals=0),
    )(where, both, mh, ml, arrow)


def rest_kernel(
    where_ref, both_ref, z_ref, diag_ref, arrow_ref, arrows_ref, out_ref, sd_ref, sa_ref, L0, L1, D1, sem
):
    copies = []

    def fetch(source, target):
        copy = pltpu.make_async_copy(source, target, sem.at[len(copies)])
        copy.start()
        copies.append(copy)

    parts = [slice(k, k + 256) for k in range(0, N, 256)]
    for part in parts:
        fetch(both_ref.at[1, part, :], L1.at[part, :])
    fetch(diag_ref.at[1], D1)
    for part in parts:
        fetch(both_ref.at[0, :, part], L0.at[:, part])
    z = z_ref[...]
    sa_ref[...] = arrows_ref[1] - dot3_t(arrow_ref[...], z[:B], z[B:])
    copies[4].wait()
    for k, part in enumerate(parts):
        copies[k].wait()
        sd_ref[:, part] = D1[:, part] - dot3_t(z, *split(L1[part, :]))
    for k, part in enumerate(parts):
        copies[5 + k].wait()
        out_ref[0, :, part] = jnp.where(where_ref[1] > 0, -dot3(z, *split(L0[:, part])), 0.0)


def rest_call(where, both, z, diag, arrow, arrows):
    return pl.pallas_call(
        rest_kernel,
        name="rest",
        out_shape=(shape(1, B, N), shape(B, N), shape(NF, B)),
        in_specs=[SMEM, ANY, VMEM, ANY, VMEM, VMEM],
        out_specs=(VMEM,) * 3,
        scratch_shapes=[
            pltpu.VMEM((N, N), F32), pltpu.VMEM((N, N), F32), pltpu.VMEM((B, N), F32),
            pltpu.SemaphoreType.DMA((9,)),
        ],
        compiler_params=params(),
        cost_estimate=pl.CostEstimate(flops=4 * 10**9, bytes_accessed=12 * 10**6, transcendentals=0),
    )(where, both, z, diag, arrow, arrows)


def pack_call(row, diag, obs, cov):
    return pl.pallas_call(
        pack_kernel,
        name="pack",
        out_shape=(shape(PIECE, B), shape(2, NF, B)),
        in_specs=[SMEM, ANY, VMEM, VMEM],
        out_specs=(VMEM, VMEM),
        scratch_shapes=[pltpu.SemaphoreType.DMA((5,))],
        compiler_params=params(),
    )(row, diag, obs, cov)


def ring(x):
    across = [(i, i ^ 1) for i in range(NB)]
    forth = [(i, (i + 2) % NB) for i in range(NB)]
    back = [(i, (i - 2) % NB) for i in range(NB)]
    send = functools.partial(lax.ppermute, axis_name="col")
    half = x.shape[0] // 2
    up = send(x, perm=forth)
    down = send(x, perm=back)
    other = send(x, perm=across)
    up2 = send(up[:half], perm=forth)
    down2 = send(down[half:], perm=back)
    o_up = send(up, perm=across)
    o_down = send(down, perm=across)
    o_up2 = send(up2, perm=across)
    o_down2 = send(down2, perm=across)
    return (x, other, up, down, o_up, o_down, up2, down2, o_up2, o_down2)


def other_half(x, k):
    return lax.ppermute(x, "tm", [(i, i ^ k) for i in range(32)])


def per_device(diag, lower, obs, cov, prior):
    col = lax.axis_index("col").astype(jnp.int32)
    tm = lax.axis_index("tm")
    where = jnp.stack([col, (tm > 0).astype(jnp.int32)])
    piece, arrows = pack_call(col[None], diag, obs, cov)
    late, piece = lax.optimization_barrier((lower, piece))
    both = lax.all_gather(late, "col", axis=1, tiled=True)
    pieces = ring(piece)
    factors, mh, ml, arrow, z, tip = factor_call(where, pieces, lower)
    term = other_half(tip, 1)
    handed = handed_call(where, both, mh, ml, arrow)
    term, handed = lax.optimization_barrier((term, handed))
    tip = tip + term
    received = lax.ppermute(handed, "tm", [(i, i - 1) for i in range(1, 32)])
    tip = tip + other_half(tip, 8)
    tip, z = lax.optimization_barrier((tip, z))
    term = other_half(tip, 16)
    coupling, pivot, arrow_cols = rest_call(where, both, z, diag, arrow, arrows)
    term, pivot, arrow_cols = lax.optimization_barrier((term, pivot, arrow_cols))
    tip = tip + term
    tip = tip + other_half(tip, 2)
    tip = tip + other_half(tip, 4)
    separator_diag = (pivot + received[:B])[None]
    separator_arrow = (arrow_cols + received[B:].reshape(8, NB, B).transpose(1, 0, 2).reshape(NF, B))[None]
    tip_block = prior + tip[:NF]
    log_pivots = tip[NF, 0] / (32 * N)
    return (factors, separator_diag, coupling, separator_arrow, tip_block, log_pivots)


def solution(mesh):
    return jax.shard_map(
        per_device,
        mesh=mesh,
        in_specs=(
            P("tm", "col", None),
            P("tm", "col", None),
            P("tm", "col"),
            P("tm", None, "col"),
            P(),
        ),
        out_specs=(
            P("tm", "col", None),
            P("tm", "col", None),
            P("tm", "col", None),
            P("tm", None, "col"),
            P(),
            P(),
        ),
        check_vma=False,
    )
```

```python
import functools

import jax
import jax.numpy as jnp
from jax import lax
from jax.experimental import pallas as pl
from jax.experimental.pallas import tpu as pltpu
from jax.sharding import PartitionSpec as P

B = 128
NB = 8
N = B * NB
NF = 64
PIECE = 6 * B
F32 = jnp.float32
BF16 = jnp.bfloat16
VMEM = pl.BlockSpec(memory_space=pltpu.VMEM)
SMEM = pl.BlockSpec(memory_space=pltpu.SMEM)
ANY = pl.BlockSpec(memory_space=pl.ANY)


def params():
    return pltpu.CompilerParams(vmem_limit_bytes=56 * 2**20)


def shape(*dims, dtype=F32):
    return jax.ShapeDtypeStruct(dims, dtype)


def split(x):
    high = x.astype(BF16)
    return high, (x - high.astype(F32)).astype(BF16)


def dot(a, b):
    return jnp.dot(a, b, preferred_element_type=F32)


def dot_t(a, b):
    return lax.dot_general(a, b, (((1,), (1,)), ((), ())), preferred_element_type=F32)


def stack(x):
    return jnp.concatenate(split(x), axis=0)


def dot3(a, bh, bl):
    rows = a.shape[0] // 2
    both = dot(a, bh)
    return both[:rows] + (both[rows:] + dot(a[:rows], bl))


def dot3_t(a, bh, bl):
    rows = a.shape[0] // 2
    both = dot_t(a, bh)
    return both[:rows] + (both[rows:] + dot_t(a[:rows], bl))


def block(index):
    return pl.ds(pl.multiple_of(index * B, B), B)


def sent_columns(row):
    chip = row // 2
    following = (chip + 1) % 4
    across = (row + 4) % NB
    flipped = across + 1 - 2 * (across % 2)
    last = across + (flipped - across) * (chip // 2)
    return [2 * chip, 2 * chip + 1, 2 * following, 2 * following + 1, last]


def pack_kernel(row_ref, diag_ref, obs_ref, cov_ref, piece_ref, arrows_ref, sem):
    copies = []
    for slot, column in enumerate(sent_columns(row_ref[0])):
        copy = pltpu.make_async_copy(
            diag_ref.at[0, :, block(column)], piece_ref.at[slot * B : (slot + 1) * B, :], sem.at[slot]
        )
        copy.start()
        copies.append(copy)
    tip = jnp.zeros((NF, NF), F32)
    for t in range(2):
        cov = cov_ref[t]
        arrow = cov * obs_ref[t : t + 1, :]
        arrows_ref[t] = arrow
        if t == 0:
            piece_ref[5 * B : 5 * B + NF, :] = arrow
        tip = tip + dot3_t(stack(arrow), *split(cov))
    piece_ref[5 * B + NF :, :] = jnp.concatenate([tip, jnp.zeros((NF, B - NF), F32)], axis=1)
    for copy in copies:
        copy.wait()


def diag_factor(S, between):
    lane = lax.broadcasted_iota(jnp.int32, (8, B), 1)
    sub = lax.broadcasted_iota(jnp.int32, (8, B), 0)
    H = B // 2
    Sv = [S[8 * v : 8 * v + 8, :] for v in range(B // 8)]
    X, FD, SC = [], [], []

    def over_lanes(x, i):
        return jnp.broadcast_to(x[:, i : i + 1], (8, B))

    def over_rows(x, j):
        return jnp.broadcast_to(x[j : j + 1, :], (8, B))

    for g in range(B // 8):
        base = 8 * g
        end = 8 if g < 8 else 16
        if g == 8:
            top = jnp.concatenate(X, axis=0)
            lane_h = lax.broadcasted_iota(jnp.int32, (H, B), 1)
            sub_h = lax.broadcasted_iota(jnp.int32, (H, B), 0)
            kept = jnp.where((lane_h >= H) | (lane_h // 8 <= sub_h // 8), top, 0.0)
            kh, kl = split(kept)
            fh, fl = split(top[:, H:].T)
            product = dot(jnp.concatenate([fh, fl, fh], axis=1), jnp.concatenate([kh, kh, kl], axis=0))
            for v in range(8, 16):
                rows = product[8 * v - H : 8 * v - H + 8, :]
                Sv[v] = jnp.where(lane >= H, Sv[v], 0.0) - rows
        if g % 8 == 0:
            C = [over_lanes(Sv[g], base + i) for i in range(8)]
        Ct = {v: [over_lanes(Sv[v], base + i) for i in range(8)] for v in range(g + 1, end) if v > g + 1 or g % 8 == 0}
        if g % 8 > 0 and g + 1 < end:
            Ct[g + 1] = second
        second = [over_lanes(Sv[g + 2], base + 8 + i) for i in range(8)] if g + 2 < end else None
        ahead = [over_lanes(Sv[g + 1], base + 8 + i) for i in range(8)] if g + 1 < end else None
        inside = (lane >= base) & (lane < base + 8)
        R = jnp.where(inside, (lane == base + sub).astype(F32), Sv[g])
        Rt = {v: jnp.where(inside, 0.0, Sv[v]) for v in range(g + 1, end)}
        scale = None
        fd = None
        rj, rows = [], []
        for j in range(8):
            d = over_rows(C[j], j)
            r = 1.0 / d
            rs = lax.rsqrt(d)
            fc = C[j] * rs
            fd = fc if fd is None else jnp.where(lane == base + j, fc, fd)
            scale = rs if scale is None else jnp.where(sub == j, rs, scale)
            rj.append(r)
            rows.append(over_rows(R, j))
            if j < 7:
                m = jnp.where(sub > j, C[j] * r, 0.0)
                R = R - m * rows[j]
                for i in range(j + 1, 8):
                    C[i] = C[i] - m * over_rows(C[j], i)
        for v in range(g + 1, end):
            for j in range(8):
                mt = Ct[v][j] * rj[j]
                if v == g + 1:
                    for i in range(8):
                        ahead[i] = ahead[i] - mt * over_rows(Ct[v][j], i)
                if v == g + 2:
                    for i in range(8):
                        second[i] = second[i] - mt * over_rows(Ct[g + 1][j], i)
                Rt[v] = Rt[v] - mt * rows[j]
                for i in range(j + 1, 8):
                    Ct[v][i] = Ct[v][i] - mt * over_rows(C[j], i)
        for v in range(g + 1, end):
            Sv[v] = Rt[v]
        C = ahead
        X.append(R * scale)
        FD.append(jnp.where(inside & (lane <= base + sub), fd, 0.0))
        SC.append(scale)
        between(g)
    return X, FD, SC


def place_piece(source, slot_base, slots, row, D, sem, base):
    copies = []
    columns = sent_columns(row)
    for k in range(slots):
        slot = slot_base + k
        if slot < 5:
            copy = pltpu.make_async_copy(
                source.at[k * B : (k + 1) * B, :], D.at[block(row), block(columns[slot])], sem.at[base + k]
            )
            copy.start()
            copies.append(copy)
    return copies


def factor_kernel(
    where_ref, own, other, up, down, o_up, o_down, up2, down2, o_up2, o_down2, lower_ref,
    f_ref, mh_ref, ml_ref, arrow_ref, z_ref, tip_ref,
    D, A, T, Fs, F2, Uh, Ul, Mh, Ml, W, P, L1, G, Z, sem, sem2, sem3,
):
    row = where_ref[0]
    chip = row // 2
    core = row % 2

    def index(distance, same):
        c = lax.rem(chip + distance + 4, 4)
        return 2 * c + (core if same else 1 - core)

    sources = [
        (own, 0, 6, index(0, True)), (other, 0, 6, index(0, False)),
        (up, 0, 6, index(-1, True)), (down, 0, 6, index(1, True)),
        (o_up, 0, 6, index(-1, False)), (o_down, 0, 6, index(1, False)),
        (up2, 0, 3, index(2, True)), (down2, 3, 3, index(2, True)),
        (o_up2, 0, 3, index(2, False)), (o_down2, 3, 3, index(2, False)),
    ]
    copies = []
    count = 0
    for ref, first, slots, r in sources:
        copies += place_piece(ref, first, slots, r, D, sem, count)
        count += slots
        if first + slots == 6:
            tail = (slots - 1) * B
            copy = pltpu.make_async_copy(ref.at[tail : tail + NF, :], A.at[:, block(r)], sem2.at[count])
            copy.start()
            copies.append(copy)
            copy = pltpu.make_async_copy(ref.at[tail + NF : tail + B, :], T.at[r], sem2.at[count + 1])
            copy.start()
            copies.append(copy)

    copy = pltpu.make_async_copy(lower_ref.at[1], L1, sem2.at[0])
    copy.start()
    copies.append(copy)

    lane = lax.broadcasted_iota(jnp.int32, (8, B), 1)
    lane_b = lax.broadcasted_iota(jnp.int32, (B, B), 1)
    sub_b = lax.broadcasted_iota(jnp.int32, (B, B), 0)
    inverse_part = (lane_b // 8) <= (sub_b // 8)
    for b in range(0, NB, 2):
        corner = (slice(b * B, b * B + B), slice(b * B + B, b * B + 2 * B))
        Mh[corner] = jnp.zeros((B, B), BF16)
        Ml[corner] = jnp.zeros((B, B), BF16)
    acc = jnp.ones((8, B), F32)
    for copy in copies:
        copy.wait()
    stores = []
    tips = [sum(T[r, :, 0:NF] for r in range(NB))]
    S = D[0:B, 0:B]

    def split_rows():
        a2 = stack(A[...])
        arrow_ref[...] = a2
        nh, nl = split(L1[...])
        G[0:B, :] = nh
        G[B : B + NF, :] = a2[0:NF]
        G[B + NF : 2 * B + NF, :] = nl
        G[2 * B + NF :, :] = a2[NF:]
        Z[...] = jnp.zeros_like(Z)

    def mirror(a, b):
        D[a * B : (a + 1) * B, b * B : (b + 1) * B] = D[b * B : (b + 1) * B, a * B : (a + 1) * B].T

    def first_row():
        W[0:B, :] = D[0:B, :]

    deferred = []
    for b in range(2, NB):
        if b // 2 == 3:
            deferred += [functools.partial(mirror, a, b) for a in range(2)]
        if b // 2 >= 2:
            deferred.append(functools.partial(mirror, ((b + 4) % NB) ^ 1, b))
    deferred += [first_row, split_rows]
    for J in range(NB):
        r0 = J * B
        r1 = r0 + B
        r2 = r1 + B
        here = slice((J % 2) * B, (J % 2) * B + B)
        there = slice(((J + 1) % 2) * B, ((J + 1) % 2) * B + B)
        per_group = -(-len(deferred) // 14)

        def between(g):
            for work in deferred[:per_group]:
                work()
            del deferred[:per_group]

        X, FD, SC = diag_factor(S, between)
        for g in range(16):
            acc = jnp.where(lane == J * 16 + g, SC[g], acc)
        X = jnp.concatenate(X, 0)
        FD = jnp.concatenate(FD, 0)
        mjh, mjl = split(jnp.where(inverse_part, X, 0.0))
        mj = jnp.concatenate([mjh, mjl], axis=0)
        Mh[r0:r1, r0:r1] = mjh
        Ml[r0:r1, r0:r1] = mjl
        Fs[r0:r1, r0:r1] = jnp.where(inverse_part, 0.0, X).T + FD

        def keep_columns(w, c, r0=r0, r1=r1):
            wh, wl = split(w)
            e = c + w.shape[1]
            Uh[r0:r1, c:e] = wh
            Ul[r0:r1, c:e] = wl
            f = w.T
            Fs[c:e, r0:r1] = f
            fh, fl = split(f)
            for K in range(c // B, e // B):
                o = K * B - c
                F2[2 * K * B : 2 * K * B + B, r0:r1] = fh[o : o + B]
                F2[2 * K * B + B : 2 * K * B + 2 * B, r0:r1] = fl[o : o + B]
            return jnp.concatenate([fh[0:B], fl[0:B]], axis=0), wh, wl

        def columns(c, e, J=J, here=here, mj=mj, keep_columns=keep_columns):
            keep_columns(dot3(mj, *split(W[here, c:e])), c)

        def inverse_row(c, e, r0=r0, r1=r1, here=here, mj=mj):
            wh, wl = split(dot3(mj, *split(W[here, c:e])))
            Mh[r0:r1, c:e] = wh
            Ml[r0:r1, c:e] = wl

        def store_row(J=J, r0=r0, r1=r1):
            width = r1 + B * ((J + 1) % 2)
            for k, (source, target) in enumerate(((Mh, mh_ref), (Ml, ml_ref))):
                copy = pltpu.make_async_copy(
                    source.at[r0:r1, 0:width], target.at[r0:r1, 0:width], sem3.at[2 * J + k]
                )
                copy.start()
                stores.append(copy)

        def solve_rows(r1=r1):
            pair = slice(r1 - 2 * B, r1)
            y = dot3_t(G[:, 0:r1], Mh[pair, 0:r1], Ml[pair, 0:r1])
            arrow = y[B:]
            tips.append(-dot3_t(stack(arrow), *split(arrow)))
            Z[:, 0:r1] = Z[:, 0:r1] + dot3(stack(y[0:B]), Mh[pair, 0:r1], Ml[pair, 0:r1])

        def next_row(c, e, r1=r1, r2=r2, there=there):
            coming = slice(2 * r1, 2 * r2)
            if c >= r1:
                W[there, c:e] = D[r1:r2, c:e] - dot3(F2[coming, 0:r1], Uh[0:r1, c:e], Ul[0:r1, c:e])
            else:
                W[there, c:e] = -dot3(F2[coming, c:r1], Mh[c:r1, c:e], Ml[c:r1, c:e])

        def pieces_of(c, e):
            while c < e:
                stop = min(e, c - c % 256 + 256)
                yield c, stop
                c = stop

        def partial_pivot(r1=r1, r2=r2, J=J):
            P[...] = D[r2 : r2 + B, r2 : r2 + B] - dot3(
                F2[2 * r2 : 2 * r2 + 2 * B, 0:r1], Uh[0:r1, r2 : r2 + B], Ul[0:r1, r2 : r2 + B]
            )

        if J + 1 < NB:
            f2, wh, wl = keep_columns(dot3(mj, *split(W[here, r1:r2])), r1)
            base = P[...] if J > 0 else D[r1:r2, r1:r2]
            S = base - dot3(f2, wh, wl)
        for c, e in pieces_of(r2, N):
            deferred.append(functools.partial(columns, c, e))
        if J + 2 < NB:
            deferred.append(partial_pivot)
            for c, e in pieces_of(r2, N):
                deferred.append(functools.partial(next_row, c, e))
        for c, e in pieces_of(0, r0):
            deferred.append(functools.partial(inverse_row, c, e))
        deferred.append(store_row)
        if J % 2 == 1:
            solves = [solve_rows]
        else:
            solves = []
        if J + 1 < NB:
            for c, e in pieces_of(0, r1):
                deferred.append(functools.partial(next_row, c, e))
        deferred += solves
    for work in deferred:
        work()
    z_ref[...] = stack(Z[...])
    tip = sum(tips)
    logs = jnp.broadcast_to(-jnp.sum(jnp.log(acc)), (8, NF))
    tip_ref[...] = jnp.concatenate([tip, logs], axis=0)
    for b in range(NB):
        cs = slice(b * B, b * B + B)
        f_ref[0, :, cs] = jnp.where(b <= row, Fs[block(row), cs], 0.0)
    for copy in stores:
        copy.wait()


def factor_call(where, pieces, lower):
    return pl.pallas_call(
        factor_kernel,
        name="factor",
        out_shape=(
            shape(1, B, N), shape(N, N, dtype=BF16), shape(N, N, dtype=BF16),
            shape(2 * NF, N, dtype=BF16), shape(2 * B, N, dtype=BF16), shape(NF + 8, NF),
        ),
        in_specs=[SMEM] + [ANY] * 11,
        out_specs=(VMEM, ANY, ANY, VMEM, VMEM, VMEM),
        scratch_shapes=[
            pltpu.VMEM((N, N), F32), pltpu.VMEM((NF, N), F32), pltpu.VMEM((NB, NF, B), F32),
            pltpu.VMEM((N, N), F32), pltpu.VMEM((2 * N, N), BF16),
        ]
        + [pltpu.VMEM((N, N), BF16)] * 4
        + [
            pltpu.VMEM((2 * B, N), F32), pltpu.VMEM((B, B), F32), pltpu.VMEM((B, N), F32),
            pltpu.VMEM((2 * B + 2 * NF, N), BF16), pltpu.VMEM((B, N), F32),
            pltpu.SemaphoreType.DMA((64,)), pltpu.SemaphoreType.DMA((64,)), pltpu.SemaphoreType.DMA((16,)),
        ],
        compiler_params=params(),
        cost_estimate=pl.CostEstimate(flops=40 * 10**9, bytes_accessed=2 * 10**7, transcendentals=0),
    )(where, *pieces, lower)


def fetch_inverse(mh_ref, ml_ref, Mh, Ml, sem):
    copies = []
    for j in range(4):
        area = (slice(j * 256, j * 256 + 256), slice(0, j * 256 + 256))
        for k, (source, target) in enumerate(((mh_ref, Mh), (ml_ref, Ml))):
            copy = pltpu.make_async_copy(source.at[area], target.at[area], sem.at[2 * j + k])
            copy.start()
            copies.append(copy)
    return copies


def solved(a, Mh, Ml, copies):
    y = []
    for k, j in enumerate(range(0, N, 256)):
        copies[2 * k].wait()
        copies[2 * k + 1].wait()
        y.append(stack(dot3_t(a[:, 0 : j + 256], Mh[j : j + 256, 0 : j + 256], Ml[j : j + 256, 0 : j + 256])))
    y = jnp.concatenate(y, axis=1)
    z = [
        stack(dot3(y[:, k:], Mh[k:, k : k + 256], Ml[k:, k : k + 256])) for k in range(0, N, 256)
    ]
    return jnp.concatenate(z, axis=1)


def handed_kernel(where_ref, both_ref, mh_ref, ml_ref, arrow_ref, out_ref, C, L, Mh, Ml, sem):
    columns = pltpu.make_async_copy(both_ref.at[0, :, block(where_ref[0])], C, sem.at[8])
    columns.start()
    copies = fetch_inverse(mh_ref, ml_ref, Mh, Ml, sem)
    whole = pltpu.make_async_copy(both_ref.at[0], L, sem.at[9])
    whole.start()
    columns.wait()
    z = solved(stack(C[...].T), Mh, Ml, copies)
    arrow = -dot3_t(arrow_ref[...], z[:B], z[B:])
    for k in range(NF // 8):
        out_ref[B:, k * B : (k + 1) * B] = arrow[8 * k : 8 * k + 8, :]
    whole.wait()
    for c in range(0, N, 256):
        out_ref[0:B, c : c + 256] = -dot3(z, *split(L[:, c : c + 256]))


def handed_call(where, both, mh, ml, arrow):
    return pl.pallas_call(
        handed_kernel,
        name="handed",
        out_shape=shape(B + 8, N),
        in_specs=[SMEM, ANY, ANY, ANY, VMEM],
        out_specs=VMEM,
        scratch_shapes=[
            pltpu.VMEM((N, B), F32), pltpu.VMEM((N, N), F32), pltpu.VMEM((N, N), BF16),
            pltpu.VMEM((N, N), BF16), pltpu.SemaphoreType.DMA((10,)),
        ],
        compiler_params=params(),
        cost_estimate=pl.CostEstimate(flops=4 * 10**9, bytes_accessed=10**7, transcendentals=0),
    )(where, both, mh, ml, arrow)


def rest_kernel(
    where_ref, both_ref, z_ref, diag_ref, arrow_ref, arrows_ref, out_ref, sd_ref, sa_ref, L0, L1, D1, sem
):
    copies = []

    def fetch(source, target):
        copy = pltpu.make_async_copy(source, target, sem.at[len(copies)])
        copy.start()
        copies.append(copy)

    parts = [slice(k, k + 256) for k in range(0, N, 256)]
    for part in parts:
        fetch(both_ref.at[1, part, :], L1.at[part, :])
    fetch(diag_ref.at[1], D1)
    for part in parts:
        fetch(both_ref.at[0, :, part], L0.at[:, part])
    z = z_ref[...]
    sa_ref[...] = arrows_ref[1] - dot3_t(arrow_ref[...], z[:B], z[B:])
    for copy in copies[:5]:
        copy.wait()
    for part in parts:
        sd_ref[:, part] = D1[:, part] - dot3_t(z, *split(L1[part, :]))
    for copy in copies[5:]:
        copy.wait()
    for part in parts:
        out_ref[0, :, part] = jnp.where(where_ref[1] > 0, -dot3(z, *split(L0[:, part])), 0.0)


def rest_call(where, both, z, diag, arrow, arrows):
    return pl.pallas_call(
        rest_kernel,
        name="rest",
        out_shape=(shape(1, B, N), shape(B, N), shape(NF, B)),
        in_specs=[SMEM, ANY, VMEM, ANY, VMEM, VMEM],
        out_specs=(VMEM,) * 3,
        scratch_shapes=[
            pltpu.VMEM((N, N), F32), pltpu.VMEM((N, N), F32), pltpu.VMEM((B, N), F32),
            pltpu.SemaphoreType.DMA((9,)),
        ],
        compiler_params=params(),
        cost_estimate=pl.CostEstimate(flops=80 * 10**9, bytes_accessed=200 * 10**6, transcendentals=0),
    )(where, both, z, diag, arrow, arrows)


def pack_call(row, diag, obs, cov):
    return pl.pallas_call(
        pack_kernel,
        name="pack",
        out_shape=(shape(PIECE, B), shape(2, NF, B)),
        in_specs=[SMEM, ANY, VMEM, VMEM],
        out_specs=(VMEM, VMEM),
        scratch_shapes=[pltpu.SemaphoreType.DMA((5,))],
        compiler_params=params(),
    )(row, diag, obs, cov)


def ring(x):
    across = [(i, i ^ 1) for i in range(NB)]
    forth = [(i, (i + 2) % NB) for i in range(NB)]
    back = [(i, (i - 2) % NB) for i in range(NB)]
    send = functools.partial(lax.ppermute, axis_name="col")
    half = x.shape[0] // 2
    up = send(x, perm=forth)
    down = send(x, perm=back)
    other = send(x, perm=across)
    up2 = send(up[:half], perm=forth)
    down2 = send(down[half:], perm=back)
    o_up = send(up, perm=across)
    o_down = send(down, perm=across)
    o_up2 = send(up2, perm=across)
    o_down2 = send(down2, perm=across)
    return (x, other, up, down, o_up, o_down, up2, down2, o_up2, o_down2)


def other_half(x, k):
    return lax.ppermute(x, "tm", [(i, i ^ k) for i in range(32)])


def per_device(diag, lower, obs, cov, prior):
    col = lax.axis_index("col").astype(jnp.int32)
    tm = lax.axis_index("tm")
    where = jnp.stack([col, (tm > 0).astype(jnp.int32)])
    piece, arrows = pack_call(col[None], diag, obs, cov)
    late, piece = lax.optimization_barrier((lower, piece))
    both = lax.all_gather(late, "col", axis=1, tiled=True)
    pieces = ring(piece)
    factors, mh, ml, arrow, z, tip = factor_call(where, pieces, lower)
    term = other_half(tip, 1)
    handed = handed_call(where, both, mh, ml, arrow)
    term, handed = lax.optimization_barrier((term, handed))
    tip = tip + term
    tip = tip + other_half(tip, 8)
    tip, z, handed = lax.optimization_barrier((tip, z, handed))
    term = other_half(tip, 16)
    received = lax.ppermute(handed, "tm", [(i, i - 1) for i in range(1, 32)])
    coupling, pivot, arrow_cols = rest_call(where, both, z, diag, arrow, arrows)
    term, pivot, arrow_cols = lax.optimization_barrier((term, pivot, arrow_cols))
    tip = tip + term
    tip = tip + other_half(tip, 2)
    term = other_half(tip, 4)
    separator_diag = (pivot + received[:B])[None]
    separator_arrow = (arrow_cols + received[B:].reshape(8, NB, B).transpose(1, 0, 2).reshape(NF, B))[None]
    term, separator_diag, separator_arrow = lax.optimization_barrier((term, separator_diag, separator_arrow))
    tip = tip + term
    tip_block = prior + tip[:NF]
    log_pivots = tip[NF, 0] / (32 * N)
    return (factors, separator_diag, coupling, separator_arrow, tip_block, log_pivots)


def solution(mesh):
    return jax.shard_map(
        per_device,
        mesh=mesh,
        in_specs=(
            P("tm", "col", None),
            P("tm", "col", None),
            P("tm", "col"),
            P("tm", None, "col"),
            P(),
        ),
        out_specs=(
            P("tm", "col", None),
            P("tm", "col", None),
            P("tm", "col", None),
            P("tm", None, "col"),
            P(),
            P(),
        ),
        check_vma=False,
    )
```

```python
import functools

import jax
import jax.numpy as jnp
from jax import lax
from jax.experimental import pallas as pl
from jax.experimental.pallas import tpu as pltpu
from jax.sharding import PartitionSpec as P

B = 128
NB = 8
N = B * NB
NF = 64
PIECE = 6 * B
F32 = jnp.float32
BF16 = jnp.bfloat16
VMEM = pl.BlockSpec(memory_space=pltpu.VMEM)
SMEM = pl.BlockSpec(memory_space=pltpu.SMEM)
ANY = pl.BlockSpec(memory_space=pl.ANY)


def params():
    return pltpu.CompilerParams(vmem_limit_bytes=56 * 2**20)


def shape(*dims, dtype=F32):
    return jax.ShapeDtypeStruct(dims, dtype)


def split(x):
    high = x.astype(BF16)
    return high, (x - high.astype(F32)).astype(BF16)


def dot(a, b):
    return jnp.dot(a, b, preferred_element_type=F32)


def dot_t(a, b):
    return lax.dot_general(a, b, (((1,), (1,)), ((), ())), preferred_element_type=F32)


def stack(x):
    return jnp.concatenate(split(x), axis=0)


def dot3(a, bh, bl):
    rows = a.shape[0] // 2
    both = dot(a, bh)
    return both[:rows] + (both[rows:] + dot(a[:rows], bl))


def dot3_t(a, bh, bl):
    rows = a.shape[0] // 2
    both = dot_t(a, bh)
    return both[:rows] + (both[rows:] + dot_t(a[:rows], bl))


def block(index):
    return pl.ds(pl.multiple_of(index * B, B), B)


def sent_columns(row):
    chip = row // 2
    following = (chip + 1) % 4
    across = (row + 4) % NB
    flipped = across + 1 - 2 * (across % 2)
    last = across + (flipped - across) * (chip // 2)
    return [2 * chip, 2 * chip + 1, 2 * following, 2 * following + 1, last]


def pack_kernel(row_ref, diag_ref, obs_ref, cov_ref, piece_ref, arrows_ref, sem):
    copies = []
    for slot, column in enumerate(sent_columns(row_ref[0])):
        copy = pltpu.make_async_copy(
            diag_ref.at[0, :, block(column)], piece_ref.at[slot * B : (slot + 1) * B, :], sem.at[slot]
        )
        copy.start()
        copies.append(copy)
    tip = jnp.zeros((NF, NF), F32)
    for t in range(2):
        cov = cov_ref[t]
        arrow = cov * obs_ref[t : t + 1, :]
        arrows_ref[t] = arrow
        if t == 0:
            piece_ref[5 * B : 5 * B + NF, :] = arrow
        tip = tip + dot3_t(stack(arrow), *split(cov))
    piece_ref[5 * B + NF :, :] = jnp.concatenate([tip, jnp.zeros((NF, B - NF), F32)], axis=1)
    for copy in copies:
        copy.wait()


def diag_factor(S, between):
    lane = lax.broadcasted_iota(jnp.int32, (8, B), 1)
    sub = lax.broadcasted_iota(jnp.int32, (8, B), 0)
    H = B // 2
    Sv = [S[8 * v : 8 * v + 8, :] for v in range(B // 8)]
    X, FD, SC = [], [], []

    def over_lanes(x, i):
        return jnp.broadcast_to(x[:, i : i + 1], (8, B))

    def over_rows(x, j):
        return jnp.broadcast_to(x[j : j + 1, :], (8, B))

    for g in range(B // 8):
        base = 8 * g
        end = 8 if g < 8 else 16
        if g == 8:
            top = jnp.concatenate(X, axis=0)
            lane_h = lax.broadcasted_iota(jnp.int32, (H, B), 1)
            sub_h = lax.broadcasted_iota(jnp.int32, (H, B), 0)
            kept = jnp.where((lane_h >= H) | (lane_h // 8 <= sub_h // 8), top, 0.0)
            kh, kl = split(kept)
            fh, fl = split(top[:, H:].T)
            product = dot(jnp.concatenate([fh, fl, fh], axis=1), jnp.concatenate([kh, kh, kl], axis=0))
            for v in range(8, 16):
                rows = product[8 * v - H : 8 * v - H + 8, :]
                Sv[v] = jnp.where(lane >= H, Sv[v], 0.0) - rows
        if g % 8 == 0:
            C = [over_lanes(Sv[g], base + i) for i in range(8)]
        Ct = {v: [over_lanes(Sv[v], base + i) for i in range(8)] for v in range(g + 1, end) if v > g + 1 or g % 8 == 0}
        if g % 8 > 0 and g + 1 < end:
            Ct[g + 1] = second
        second = [over_lanes(Sv[g + 2], base + 8 + i) for i in range(8)] if g + 2 < end else None
        ahead = [over_lanes(Sv[g + 1], base + 8 + i) for i in range(8)] if g + 1 < end else None
        inside = (lane >= base) & (lane < base + 8)
        R = jnp.where(inside, (lane == base + sub).astype(F32), Sv[g])
        Rt = {v: jnp.where(inside, 0.0, Sv[v]) for v in range(g + 1, end)}
        scale = None
        fd = None
        rj, rows = [], []
        for j in range(8):
            d = over_rows(C[j], j)
            r = 1.0 / d
            rs = lax.rsqrt(d)
            fc = C[j] * rs
            fd = fc if fd is None else jnp.where(lane == base + j, fc, fd)
            scale = rs if scale is None else jnp.where(sub == j, rs, scale)
            rj.append(r)
            rows.append(over_rows(R, j))
            if j < 7:
                m = jnp.where(sub > j, C[j] * r, 0.0)
                R = R - m * rows[j]
                for i in range(j + 1, 8):
                    C[i] = C[i] - m * over_rows(C[j], i)
        for v in range(g + 1, end):
            for j in range(8):
                mt = Ct[v][j] * rj[j]
                if v == g + 1:
                    for i in range(8):
                        ahead[i] = ahead[i] - mt * over_rows(Ct[v][j], i)
                if v == g + 2:
                    for i in range(8):
                        second[i] = second[i] - mt * over_rows(Ct[g + 1][j], i)
                Rt[v] = Rt[v] - mt * rows[j]
                for i in range(j + 1, 8):
                    Ct[v][i] = Ct[v][i] - mt * over_rows(C[j], i)
        for v in range(g + 1, end):
            Sv[v] = Rt[v]
        C = ahead
        X.append(R * scale)
        FD.append(jnp.where(inside & (lane <= base + sub), fd, 0.0))
        SC.append(scale)
        between(g)
    return X, FD, SC


def place_piece(source, slot_base, slots, row, D, sem, base):
    copies = []
    columns = sent_columns(row)
    for k in range(slots):
        slot = slot_base + k
        if slot < 5:
            copy = pltpu.make_async_copy(
                source.at[k * B : (k + 1) * B, :], D.at[block(row), block(columns[slot])], sem.at[base + k]
            )
            copy.start()
            copies.append(copy)
    return copies


def factor_kernel(
    where_ref, own, other, up, down, o_up, o_down, up2, down2, o_up2, o_down2, lower_ref,
    f_ref, mh_ref, ml_ref, arrow_ref, z_ref, tip_ref,
    D, A, T, Fs, F2, Uh, Ul, Mh, Ml, W, P, L1, G, Z, sem, sem2, sem3,
):
    row = where_ref[0]
    chip = row // 2
    core = row % 2

    def index(distance, same):
        c = lax.rem(chip + distance + 4, 4)
        return 2 * c + (core if same else 1 - core)

    sources = [
        (own, 0, 6, index(0, True)), (other, 0, 6, index(0, False)),
        (up, 0, 6, index(-1, True)), (down, 0, 6, index(1, True)),
        (o_up, 0, 6, index(-1, False)), (o_down, 0, 6, index(1, False)),
        (up2, 0, 3, index(2, True)), (down2, 3, 3, index(2, True)),
        (o_up2, 0, 3, index(2, False)), (o_down2, 3, 3, index(2, False)),
    ]
    copies = []
    count = 0
    for ref, first, slots, r in sources:
        copies += place_piece(ref, first, slots, r, D, sem, count)
        count += slots
        if first + slots == 6:
            tail = (slots - 1) * B
            copy = pltpu.make_async_copy(ref.at[tail : tail + NF, :], A.at[:, block(r)], sem2.at[count])
            copy.start()
            copies.append(copy)
            copy = pltpu.make_async_copy(ref.at[tail + NF : tail + B, :], T.at[r], sem2.at[count + 1])
            copy.start()
            copies.append(copy)

    copy = pltpu.make_async_copy(lower_ref.at[1], L1, sem2.at[0])
    copy.start()
    copies.append(copy)

    lane = lax.broadcasted_iota(jnp.int32, (8, B), 1)
    lane_b = lax.broadcasted_iota(jnp.int32, (B, B), 1)
    sub_b = lax.broadcasted_iota(jnp.int32, (B, B), 0)
    inverse_part = (lane_b // 8) <= (sub_b // 8)
    for b in range(0, NB, 2):
        corner = (slice(b * B, b * B + B), slice(b * B + B, b * B + 2 * B))
        Mh[corner] = jnp.zeros((B, B), BF16)
        Ml[corner] = jnp.zeros((B, B), BF16)
    acc = jnp.ones((8, B), F32)
    for copy in copies:
        copy.wait()
    stores = []
    tips = [sum(T[r, :, 0:NF] for r in range(NB))]
    S = D[0:B, 0:B]

    def split_rows():
        a2 = stack(A[...])
        arrow_ref[...] = a2
        nh, nl = split(L1[...])
        G[0:B, :] = nh
        G[B : B + NF, :] = a2[0:NF]
        G[B + NF : 2 * B + NF, :] = nl
        G[2 * B + NF :, :] = a2[NF:]
        Z[...] = jnp.zeros_like(Z)

    def mirror(a, b):
        D[a * B : (a + 1) * B, b * B : (b + 1) * B] = D[b * B : (b + 1) * B, a * B : (a + 1) * B].T

    def first_row():
        W[0:B, :] = D[0:B, :]

    deferred = []
    for b in range(2, NB):
        if b // 2 == 3:
            deferred += [functools.partial(mirror, a, b) for a in range(2)]
        if b // 2 >= 2:
            deferred.append(functools.partial(mirror, ((b + 4) % NB) ^ 1, b))
    deferred += [first_row, split_rows]
    for J in range(NB):
        r0 = J * B
        r1 = r0 + B
        r2 = r1 + B
        here = slice((J % 2) * B, (J % 2) * B + B)
        there = slice(((J + 1) % 2) * B, ((J + 1) % 2) * B + B)
        per_group = -(-len(deferred) // 14)

        def between(g):
            for work in deferred[:per_group]:
                work()
            del deferred[:per_group]

        X, FD, SC = diag_factor(S, between)
        for g in range(16):
            acc = jnp.where(lane == J * 16 + g, SC[g], acc)
        X = jnp.concatenate(X, 0)
        FD = jnp.concatenate(FD, 0)
        mjh, mjl = split(jnp.where(inverse_part, X, 0.0))
        mj = jnp.concatenate([mjh, mjl], axis=0)
        Mh[r0:r1, r0:r1] = mjh
        Ml[r0:r1, r0:r1] = mjl
        Fs[r0:r1, r0:r1] = jnp.where(inverse_part, 0.0, X).T + FD

        def keep_columns(w, c, r0=r0, r1=r1):
            wh, wl = split(w)
            e = c + w.shape[1]
            Uh[r0:r1, c:e] = wh
            Ul[r0:r1, c:e] = wl
            f = w.T
            Fs[c:e, r0:r1] = f
            fh, fl = split(f)
            for K in range(c // B, e // B):
                o = K * B - c
                F2[2 * K * B : 2 * K * B + B, r0:r1] = fh[o : o + B]
                F2[2 * K * B + B : 2 * K * B + 2 * B, r0:r1] = fl[o : o + B]
            return jnp.concatenate([fh[0:B], fl[0:B]], axis=0), wh, wl

        def columns(c, e, J=J, here=here, mj=mj, keep_columns=keep_columns):
            keep_columns(dot3(mj, *split(W[here, c:e])), c)

        def inverse_row(c, e, r0=r0, r1=r1, here=here, mj=mj):
            wh, wl = split(dot3(mj, *split(W[here, c:e])))
            Mh[r0:r1, c:e] = wh
            Ml[r0:r1, c:e] = wl

        def store_row(J=J, r0=r0, r1=r1):
            width = r1 + B * ((J + 1) % 2)
            for k, (source, target) in enumerate(((Mh, mh_ref), (Ml, ml_ref))):
                copy = pltpu.make_async_copy(
                    source.at[r0:r1, 0:width], target.at[r0:r1, 0:width], sem3.at[2 * J + k]
                )
                copy.start()
                stores.append(copy)

        def solve_rows(r1=r1):
            pair = slice(r1 - 2 * B, r1)
            y = dot3_t(G[:, 0:r1], Mh[pair, 0:r1], Ml[pair, 0:r1])
            arrow = y[B:]
            tips.append(-dot3_t(stack(arrow), *split(arrow)))
            Z[:, 0:r1] = Z[:, 0:r1] + dot3(stack(y[0:B]), Mh[pair, 0:r1], Ml[pair, 0:r1])

        def next_row(c, e, r1=r1, r2=r2, there=there):
            coming = slice(2 * r1, 2 * r2)
            if c >= r1:
                W[there, c:e] = D[r1:r2, c:e] - dot3(F2[coming, 0:r1], Uh[0:r1, c:e], Ul[0:r1, c:e])
            else:
                W[there, c:e] = -dot3(F2[coming, c:r1], Mh[c:r1, c:e], Ml[c:r1, c:e])

        def pieces_of(c, e):
            while c < e:
                stop = min(e, c - c % 256 + 256)
                yield c, stop
                c = stop

        def partial_pivot(r1=r1, r2=r2, J=J):
            P[...] = D[r2 : r2 + B, r2 : r2 + B] - dot3(
                F2[2 * r2 : 2 * r2 + 2 * B, 0:r1], Uh[0:r1, r2 : r2 + B], Ul[0:r1, r2 : r2 + B]
            )

        if J + 1 < NB:
            f2, wh, wl = keep_columns(dot3(mj, *split(W[here, r1:r2])), r1)
            base = P[...] if J > 0 else D[r1:r2, r1:r2]
            S = base - dot3(f2, wh, wl)
        for c, e in pieces_of(r2, N):
            deferred.append(functools.partial(columns, c, e))
        if J + 2 < NB:
            deferred.append(partial_pivot)
            for c, e in pieces_of(r2, N):
                deferred.append(functools.partial(next_row, c, e))
        for c, e in pieces_of(0, r0):
            deferred.append(functools.partial(inverse_row, c, e))
        deferred.append(store_row)
        if J % 2 == 1:
            solves = [solve_rows]
        else:
            solves = []
        if J + 1 < NB:
            for c, e in pieces_of(0, r1):
                deferred.append(functools.partial(next_row, c, e))
        deferred += solves
    for work in deferred:
        work()
    z_ref[...] = stack(Z[...])
    tip = sum(tips)
    logs = jnp.broadcast_to(-jnp.sum(jnp.log(acc)), (8, NF))
    tip_ref[...] = jnp.concatenate([tip, logs], axis=0)
    for b in range(NB):
        cs = slice(b * B, b * B + B)
        f_ref[0, :, cs] = jnp.where(b <= row, Fs[block(row), cs], 0.0)
    for copy in stores:
        copy.wait()


def factor_call(where, pieces, lower):
    return pl.pallas_call(
        factor_kernel,
        name="factor",
        out_shape=(
            shape(1, B, N), shape(N, N, dtype=BF16), shape(N, N, dtype=BF16),
            shape(2 * NF, N, dtype=BF16), shape(2 * B, N, dtype=BF16), shape(NF + 8, NF),
        ),
        in_specs=[SMEM] + [ANY] * 11,
        out_specs=(VMEM, ANY, ANY, VMEM, VMEM, VMEM),
        scratch_shapes=[
            pltpu.VMEM((N, N), F32), pltpu.VMEM((NF, N), F32), pltpu.VMEM((NB, NF, B), F32),
            pltpu.VMEM((N, N), F32), pltpu.VMEM((2 * N, N), BF16),
        ]
        + [pltpu.VMEM((N, N), BF16)] * 4
        + [
            pltpu.VMEM((2 * B, N), F32), pltpu.VMEM((B, B), F32), pltpu.VMEM((B, N), F32),
            pltpu.VMEM((2 * B + 2 * NF, N), BF16), pltpu.VMEM((B, N), F32),
            pltpu.SemaphoreType.DMA((64,)), pltpu.SemaphoreType.DMA((64,)), pltpu.SemaphoreType.DMA((16,)),
        ],
        compiler_params=params(),
        cost_estimate=pl.CostEstimate(flops=40 * 10**9, bytes_accessed=2 * 10**7, transcendentals=0),
    )(where, *pieces, lower)


def fetch_inverse(mh_ref, ml_ref, Mh, Ml, sem):
    copies = []
    for j in range(4):
        area = (slice(j * 256, j * 256 + 256), slice(0, j * 256 + 256))
        for k, (source, target) in enumerate(((mh_ref, Mh), (ml_ref, Ml))):
            copy = pltpu.make_async_copy(source.at[area], target.at[area], sem.at[2 * j + k])
            copy.start()
            copies.append(copy)
    return copies


def solved(a, Mh, Ml, copies):
    y = []
    for k, j in enumerate(range(0, N, 256)):
        copies[2 * k].wait()
        copies[2 * k + 1].wait()
        y.append(stack(dot3_t(a[:, 0 : j + 256], Mh[j : j + 256, 0 : j + 256], Ml[j : j + 256, 0 : j + 256])))
    y = jnp.concatenate(y, axis=1)
    z = [
        stack(dot3(y[:, k:], Mh[k:, k : k + 256], Ml[k:, k : k + 256])) for k in range(0, N, 256)
    ]
    return jnp.concatenate(z, axis=1)


def handed_kernel(where_ref, both_ref, mh_ref, ml_ref, arrow_ref, out_ref, C, L, Mh, Ml, sem):
    columns = pltpu.make_async_copy(both_ref.at[0, :, block(where_ref[0])], C, sem.at[8])
    columns.start()
    copies = fetch_inverse(mh_ref, ml_ref, Mh, Ml, sem)
    whole = pltpu.make_async_copy(both_ref.at[0], L, sem.at[9])
    whole.start()
    columns.wait()
    z = solved(stack(C[...].T), Mh, Ml, copies)
    arrow = -dot3_t(arrow_ref[...], z[:B], z[B:])
    for k in range(NF // 8):
        out_ref[B:, k * B : (k + 1) * B] = arrow[8 * k : 8 * k + 8, :]
    whole.wait()
    for c in range(0, N, 256):
        out_ref[0:B, c : c + 256] = -dot3(z, *split(L[:, c : c + 256]))


def handed_call(where, both, mh, ml, arrow):
    return pl.pallas_call(
        handed_kernel,
        name="handed",
        out_shape=shape(B + 8, N),
        in_specs=[SMEM, ANY, ANY, ANY, VMEM],
        out_specs=VMEM,
        scratch_shapes=[
            pltpu.VMEM((N, B), F32), pltpu.VMEM((N, N), F32), pltpu.VMEM((N, N), BF16),
            pltpu.VMEM((N, N), BF16), pltpu.SemaphoreType.DMA((10,)),
        ],
        compiler_params=params(),
        cost_estimate=pl.CostEstimate(flops=4 * 10**9, bytes_accessed=10**7, transcendentals=0),
    )(where, both, mh, ml, arrow)


def rest_kernel(
    where_ref, both_ref, z_ref, diag_ref, arrow_ref, arrows_ref, out_ref, sd_ref, sa_ref, L0, L1, D1, sem
):
    copies = []

    def fetch(source, target):
        copy = pltpu.make_async_copy(source, target, sem.at[len(copies)])
        copy.start()
        copies.append(copy)

    parts = [slice(k, k + 256) for k in range(0, N, 256)]
    for part in parts:
        fetch(both_ref.at[1, part, :], L1.at[part, :])
    fetch(diag_ref.at[1], D1)
    for part in parts:
        fetch(both_ref.at[0, :, part], L0.at[:, part])
    z = z_ref[...]
    sa_ref[...] = arrows_ref[1] - dot3_t(arrow_ref[...], z[:B], z[B:])
    for copy in copies[:5]:
        copy.wait()
    for part in parts:
        sd_ref[:, part] = D1[:, part] - dot3_t(z, *split(L1[part, :]))
    for copy in copies[5:]:
        copy.wait()
    for part in parts:
        out_ref[0, :, part] = jnp.where(where_ref[1] > 0, -dot3(z, *split(L0[:, part])), 0.0)


def rest_call(where, both, z, diag, arrow, arrows):
    return pl.pallas_call(
        rest_kernel,
        name="rest",
        out_shape=(shape(1, B, N), shape(B, N), shape(NF, B)),
        in_specs=[SMEM, ANY, VMEM, ANY, VMEM, VMEM],
        out_specs=(VMEM,) * 3,
        scratch_shapes=[
            pltpu.VMEM((N, N), F32), pltpu.VMEM((N, N), F32), pltpu.VMEM((B, N), F32),
            pltpu.SemaphoreType.DMA((9,)),
        ],
        compiler_params=params(),
        cost_estimate=pl.CostEstimate(flops=80 * 10**9, bytes_accessed=200 * 10**6, transcendentals=0),
    )(where, both, z, diag, arrow, arrows)


def pack_call(row, diag, obs, cov):
    return pl.pallas_call(
        pack_kernel,
        name="pack",
        out_shape=(shape(PIECE, B), shape(2, NF, B)),
        in_specs=[SMEM, ANY, VMEM, VMEM],
        out_specs=(VMEM, VMEM),
        scratch_shapes=[pltpu.SemaphoreType.DMA((5,))],
        compiler_params=params(),
    )(row, diag, obs, cov)


def ring(x):
    across = [(i, i ^ 1) for i in range(NB)]
    forth = [(i, (i + 2) % NB) for i in range(NB)]
    back = [(i, (i - 2) % NB) for i in range(NB)]
    send = functools.partial(lax.ppermute, axis_name="col")
    half = x.shape[0] // 2
    up = send(x, perm=forth)
    down = send(x, perm=back)
    other = send(x, perm=across)
    up2 = send(up[:half], perm=forth)
    down2 = send(down[half:], perm=back)
    o_up = send(up, perm=across)
    o_down = send(down, perm=across)
    o_up2 = send(up2, perm=across)
    o_down2 = send(down2, perm=across)
    return (x, other, up, down, o_up, o_down, up2, down2, o_up2, o_down2)


def other_half(x, k):
    return lax.ppermute(x, "tm", [(i, i ^ k) for i in range(32)])


def per_device(diag, lower, obs, cov, prior):
    col = lax.axis_index("col").astype(jnp.int32)
    tm = lax.axis_index("tm")
    where = jnp.stack([col, (tm > 0).astype(jnp.int32)])
    piece, arrows = pack_call(col[None], diag, obs, cov)
    late, piece = lax.optimization_barrier((lower, piece))
    both = lax.all_gather(late, "col", axis=1, tiled=True)
    pieces = ring(piece)
    factors, mh, ml, arrow, z, tip = factor_call(where, pieces, lower)
    term = other_half(tip, 1)
    handed = handed_call(where, both, mh, ml, arrow)
    term, handed = lax.optimization_barrier((term, handed))
    tip = tip + term
    tip = tip + other_half(tip, 8)
    tip = tip + other_half(tip, 16)
    tip, z, handed = lax.optimization_barrier((tip, z, handed))
    term = other_half(tip, 2)
    received = lax.ppermute(handed, "tm", [(i, i - 1) for i in range(1, 32)])
    coupling, pivot, arrow_cols = rest_call(where, both, z, diag, arrow, arrows)
    term, pivot, arrow_cols = lax.optimization_barrier((term, pivot, arrow_cols))
    tip = tip + term
    term = other_half(tip, 4)
    separator_diag = (pivot + received[:B])[None]
    separator_arrow = (arrow_cols + received[B:].reshape(8, NB, B).transpose(1, 0, 2).reshape(NF, B))[None]
    term, separator_diag, separator_arrow = lax.optimization_barrier((term, separator_diag, separator_arrow))
    tip = tip + term
    tip_block = prior + tip[:NF]
    log_pivots = tip[NF, 0] / (32 * N)
    return (factors, separator_diag, coupling, separator_arrow, tip_block, log_pivots)


def solution(mesh):
    return jax.shard_map(
        per_device,
        mesh=mesh,
        in_specs=(
            P("tm", "col", None),
            P("tm", "col", None),
            P("tm", "col"),
            P("tm", None, "col"),
            P(),
        ),
        out_specs=(
            P("tm", "col", None),
            P("tm", "col", None),
            P("tm", "col", None),
            P("tm", None, "col"),
            P(),
            P(),
        ),
        check_vma=False,
    )
```
